128 devices in a mesh: row: 16 (over x_lo, y, core), col: 8 (over x_hi, z).
Axes of the slice: x: 4 (x_hi: 2, x_lo: 2; x = x_hi * 2 + x_lo), y: 4, z: 4, core: 2. Of those that a mesh axis runs over, the one named last changes fastest.
Arguments:
- density: float32 [512, 12, 128, 128], P(('row', 'col')), may hold values from -0.5 to 0.5
- pattern: int32 [512, 12], replicated, may hold values from 0 to 511, as said below
- ham_strain: bfloat16 [9, 512, 12, 128, 128], P(None, ('row', 'col')), may hold values from -6 to 6
Outputs:
- purified: float32 [512, 12, 128, 128], P(('row', 'col'))
- virial: float32 [3, 3], replicated
The draws below stay inside these ranges and needn't reach their ends.
Inputs may be any that keep to these rules, and one draw needn't show every extreme that they name: Device d = r * 8 + c holds block rows d * 4 to d * 4 + 3. Row g's pattern lists 12 distinct block rows: g itself, the other rows of its device, and one row of each of the eight devices at (r + i, c + j), i and j in -1, 0, 1, not both 0, taken modulo the grid's sizes; the order within a row is arbitrary. Together the pattern rows of one device name exactly 2 distinct rows of each of its eight neighbouring devices.
All inputs are finite; a program needn't handle non-finite values.
Results may differ from the reference program's by a relative error of at most 0.0003.
Values sent between devices are 32-bit elements; how exact they have to be, the bound alone decides.
No kernel may reach another device: no remote copies, remote signals or barrier semaphores. Data moves between devices by JAX's collectives and lax.ppermute only.
A program may use at most 256 MiB of HBM per device.

```python
import jax
import jax.numpy as jnp
from jax import lax

B = 128
R = 4
CAP = 2
K = 12
NB = 512
N_ROW = 16
N_COL = 8


DIRECTIONS = ((-1, -1), (-1, 0), (-1, 1), (0, -1), (0, 1), (1, -1), (1, 0), (1, 1))


def pattern_tables(key):
    devices_all = N_ROW * N_COL
    key_sub = jax.random.fold_in(key, 11)
    key_off = jax.random.fold_in(key, 12)
    key_perm = jax.random.fold_in(key, 13)
    local = jnp.arange(R, dtype=jnp.int32)
    raw = jax.random.randint(key_sub, (devices_all, 8, R), 0, 1 << 20)
    scores = raw * R + local
    subsets = jnp.argsort(scores, axis=-1, stable=True)[:, :, :CAP].astype(jnp.int32)
    offsets = jax.random.randint(key_off, (devices_all, 8), 0, CAP).astype(jnp.int32)
    dev = jnp.arange(devices_all, dtype=jnp.int32)
    dev_row = dev // N_COL
    dev_col = dev % N_COL
    step_row = jnp.array([d[0] for d in DIRECTIONS], dtype=jnp.int32)
    step_col = jnp.array([d[1] for d in DIRECTIONS], dtype=jnp.int32)
    nbr = (dev_row[:, None] + step_row[None, :]) % N_ROW * N_COL + (dev_col[:, None] + step_col[None, :]) % N_COL
    which = (local[None, None, :] + offsets[:, :, None]) % CAP
    back = (7 - jnp.arange(8, dtype=jnp.int32))[None, :, None]
    picked = subsets[nbr[:, :, None], back, which]
    far_ids = nbr[:, :, None] * R + picked
    own_ids = dev[:, None, None] * R + (local[None, :, None] + local[None, None, :]) % R
    rows = jnp.concatenate([own_ids, jnp.transpose(far_ids, (0, 2, 1))], axis=-1).reshape(NB, K)
    pscore = jax.random.randint(key_perm, (NB, K), 0, 1 << 20) * K + jnp.arange(K, dtype=jnp.int32)
    order = jnp.argsort(pscore, axis=-1, stable=True)
    rows = jnp.take_along_axis(rows, order, axis=-1).astype(jnp.int32)
    return rows


def draw_pattern(key, part):
    return pattern_tables(key)


def steps_of(rng, shape, shards, low, largest):
    def one(position, blocks):
        heights = jax.random.uniform(jax.random.fold_in(jax.random.fold_in(rng, 6), position), (blocks,), jnp.float32, low / len(shards), largest / len(shards))
        return jnp.repeat(jnp.exp(heights), shape[position] // blocks).reshape((-1,) + (1,) * (len(shape) - position - 1))

    loudness = one(*shards[0])
    for cut in shards[1:]:
        loudness = loudness * one(*cut)
    return loudness


def scatter_about(rng, extent, deviation, bound, cuts=(), kind=jnp.bfloat16):
    values = jax.random.normal(rng, extent, jnp.float32) * deviation
    if len(cuts) > 0:
        values = steps_of(rng, extent, cuts, -0.22, 0.18) * values
    return jnp.clip(values, min=-bound, max=bound).astype(kind)


def setup_inputs(seed: int = 0) -> dict:
    key_of = jax.random.split(jax.random.key(seed), 4)
    return {
        "density": scatter_about(key_of[0], (NB, K, B, B), B ** -0.5, 0.5, ((0, 128),), jnp.float32),
        "pattern": draw_pattern(jax.random.fold_in(key_of[3], 71), 0),
        "ham_strain": scatter_about(key_of[2], (9, NB, K, B, B), 1.0, 6.0, ((1, 128),)),
    }


def reference(density, pattern, ham_strain):
    largest_index = lax.Precision.HIGHEST

    def purify(block_row_number):
        cols_row = pattern[block_row_number]
        blocks = jnp.take(density, cols_row, axis=0)
        inner = jnp.take(pattern, cols_row, axis=0)
        match = (inner[:, None, :] == cols_row[None, :, None]).astype(jnp.float32)
        chosen_entries = jnp.einsum('stu,suxy->stxy', match, blocks, precision=largest_index)
        squared_density = jnp.einsum('gkj,gfjh->fkh', density[block_row_number], chosen_entries, precision=largest_index)
        cubed_density = jnp.einsum('gkj,gfjh->fkh', squared_density, chosen_entries, precision=largest_index)
        return 3.0 * squared_density - 2.0 * cubed_density

    purified = lax.map(purify, jnp.arange(NB, dtype=jnp.int32))
    factor = 1.0 / (float(NB * K * B * B) ** 0.5)
    parts = [jnp.sum(ham_strain[comp].astype(jnp.float32) * purified) for comp in range(9)]
    virial = (jnp.stack(parts) * factor).reshape(3, 3)
    return purified, virial
```

```python
import math

import jax
import jax.numpy as jnp
from jax import lax
from jax.experimental import pallas as pl
from jax.experimental.pallas import tpu as pltpu
from jax.sharding import PartitionSpec as P

AXES = ("row", "col")
EDGE = 128
OWN = 4
SLOTS = 12
N_ROW = 16
N_COL = 8
N_DEV = N_ROW * N_COL

DIRS = ((-1, -1), (-1, 0), (-1, 1), (0, -1), (0, 1), (1, -1), (1, 0), (1, 1))


def near(a, b):
    return max(abs(a[0] - b[0]), abs(a[1] - b[1])) <= 1


COMMON = tuple(
    tuple(e for e in range(8) if e != d and near(DIRS[e], DIRS[d])) for d in range(8)
)
COUNT = tuple(2 + len(COMMON[d]) for d in range(8))
BACK = tuple(DIRS.index((dr, -dc)) for dr, dc in DIRS)
SEEN = tuple(
    tuple(
        DIRS.index(
            (
                (DIRS[e][0] - DIRS[d][0]) * (1 if DIRS[d][0] == 0 else -1),
                DIRS[e][1] - DIRS[d][1],
            )
        )
        for e in COMMON[d]
    )
    for d in range(8)
)

T_SLOT = 0
T_NAME = 48
T_LOW = 96
T_FAR = 104
T_SEND = 264
T_SIZE = 264 + 80
SEND_AT = tuple(T_SEND + 2 * sum(COUNT[:f]) for f in range(8))
CODES = tuple((dr + 1) * 3 + dc + 1 for dr, dc in DIRS)


def place(value, row, col):
    dev = value >> 2
    dr = ((dev >> 3) - row + 1) & (N_ROW - 1)
    dc = ((dev & (N_COL - 1)) - col + 1) & (N_COL - 1)
    return jnp.where(((row & 1) == 1) & (dr < 3), 2 - dr, dr), dc


def device_at(row, col, d):
    dr, dc = DIRS[d]
    towards = 1 - 2 * (row & 1)
    return ((row + dr * towards) & (N_ROW - 1)) * N_COL + ((col + dc) & (N_COL - 1))


def own_table(pat, row, col, tab):
    me = row * N_COL + col
    for l in range(OWN):
        for u in range(SLOTS):
            value = pat[u, me * OWN + l]
            dr, dc = place(value, row, col)
            code = dr * 3 + dc
            number = value & 3
            o = jnp.where(code == 4, number, code + jnp.where(code > 4, 3, 4))
            tab[T_SLOT + l * SLOTS + o] = u
            tab[T_NAME + l * SLOTS + o] = number


def named_rows(pat, other, me):
    named = []
    for j in range(OWN):
        number = jnp.int32(0)
        for u in range(SLOTS):
            value = pat[u, other * OWN + j]
            number = jnp.where((value >> 2) == me, value & 3, number)
        named.append(number)
    low = jnp.minimum(jnp.minimum(named[0], named[1]), jnp.minimum(named[2], named[3]))
    high = jnp.maximum(jnp.maximum(named[0], named[1]), jnp.maximum(named[2], named[3]))
    return low, high


def send_table(pat, row, col, tab):
    for f in range(8):
        d = BACK[f]
        rows = named_rows(pat, device_at(row, col, f), row * N_COL + col)
        for k, l in enumerate(rows):
            columns = [l, 4 + f] + [4 + e for e in SEEN[d]]
            for m, o in enumerate(columns):
                tab[SEND_AT[f] + k * COUNT[d] + m] = l * SLOTS + tab[T_SLOT + l * SLOTS + o]


def own_of(tab, f, k):
    return tab[SEND_AT[f] + k * COUNT[f] + 1]


def rest_of(tab, f, k):
    at = SEND_AT[f] + k * COUNT[f]
    return [tab[at]] + [tab[at + m] for m in range(2, COUNT[f])]


def fill(out, tab, dens, f):
    for k in range(2):
        out[k] = dens[own_of(tab, f, k)]
        for m, n in enumerate(rest_of(tab, f, k)):
            out[2 + k * (COUNT[f] - 1) + m] = dens[n]


def first_kernel(pat_in, dens_in, dens, tab, near_m, near_p, far_m, far_p, beside, pat, sem):
    load = pltpu.make_async_copy(dens_in, dens, sem.at[0])
    load.start()
    pat_load = pltpu.make_async_copy(pat_in, pat, sem.at[1])
    pat_load.start()
    pat_load.wait()
    row = lax.axis_index("row")
    col = lax.axis_index("col")
    own_table(pat, row, col, tab)
    send_table(pat, row, col, tab)
    load.wait()
    for out, f, edge in ((near_m, 5, 3), (near_p, 7, 4)):
        fill(out, tab, dens, f)
        for k in range(2):
            out[8 + k] = dens[own_of(tab, edge, k)]
    for out, f in ((far_m, 0), (far_p, 2), (beside, 1)):
        fill(out, tab, dens, f)


def second_kernel(tab, dens, behind, ahead, *refs):
    pair, late_m, late_p = refs[4:]
    fill(pair, tab, dens, 6)
    for k in range(2):
        pair[12 + k] = behind[8 + k]
        pair[14 + k] = ahead[8 + k]
    for f, out in ((3, late_m), (4, late_p)):
        for k in range(2):
            for m, n in enumerate(rest_of(tab, f, k)):
                out[5 * k + m] = dens[n]


def far_table(pat, row, col, tab):
    for d in range(8):
        names = [tab[T_NAME + l * SLOTS + 4 + d] for l in range(OWN)]
        low = jnp.minimum(jnp.minimum(names[0], names[1]), jnp.minimum(names[2], names[3]))
        high = jnp.maximum(jnp.maximum(names[0], names[1]), jnp.maximum(names[2], names[3]))
        tab[T_LOW + d] = low
        other = device_at(row, col, d)
        for k, l in enumerate((low, high)):
            for u in range(SLOTS):
                value = pat[u, other * OWN + l]
                dr, dc = place(value, row, col)
                code = jnp.where((dr < 3) & (dc < 3), dr * 3 + dc, 9)
                tab[T_FAR + (2 * d + k) * 10 + code] = value & 3


def split(value):
    high = value.astype(jnp.bfloat16)
    low = (value - high.astype(jnp.float32)).astype(jnp.bfloat16)
    return jnp.concatenate([high, low], axis=1)


def product(left, right):
    return jnp.dot(
        left, jnp.concatenate([right, right], axis=0), preferred_element_type=jnp.float32
    )


def halves(value):
    return value[:, :EDGE] + value[:, EDGE:]


def bit(tab, g, d):
    return jnp.where(tab[T_NAME + g * SLOTS + 4 + d] == tab[T_LOW + d], 0, 1)


def local_kernel(pat, dens, tab_in, ham, tab, wide, square, ham_out, zeros, sem):
    for c in range(9):
        pltpu.make_async_copy(ham.at[c], ham_out.at[c], sem.at[c]).start()
    row = lax.axis_index("row")
    col = lax.axis_index("col")
    for i in range(T_LOW):
        tab[i] = tab_in[i]
    for i in range(T_SEND, T_SIZE):
        tab[i] = tab_in[i]
    far_table(pat, row, col, tab)
    zeros[...] = jnp.zeros_like(zeros)

    def widen(i, _):
        wide[i] = split(dens[i // SLOTS * SLOTS + tab[T_SLOT + i]])
        return 0

    lax.fori_loop(0, OWN * SLOTS, widen, 0)

    def rows(g, _):
        for t in range(SLOTS):
            total = None
            for s in range(OWN):
                left = wide[g * SLOTS + s]
                if t >= OWN:
                    left = masked(same_name(tab, g, s, t), left, zeros)
                total = add(total, product(left, wide[s * SLOTS + t]))
            square[g * SLOTS + t] = halves(total)
        return 0

    lax.fori_loop(0, OWN, rows, 0)
    for c in range(9):
        pltpu.make_async_copy(ham.at[c], ham_out.at[c], sem.at[c]).wait()


def masked(match, left, zeros):
    if match is None:
        return left
    return jnp.where(match, left, zeros[...])


def same_name(tab, g, s, o):
    return bit(tab, g, o - OWN) == bit(tab, s, o - OWN)


def add(total, term):
    return term if total is None else total + term


def own_terms(tab, g, dirs):
    out = []
    for d in dirs:
        b = bit(tab, g, d)
        out.append((4 + d, tab[T_FAR + (2 * d + b) * 10 + 4], 2 * d + b))
    return out


def far_terms(tab, g, dirs, at, terms):
    for d in dirs:
        b = bit(tab, g, d)
        base = at[d] + b * (COUNT[d] - 1)
        info = T_FAR + (2 * d + b) * 10
        terms[4 + d].append((4 + d, None, base))
        for j, e in enumerate(COMMON[d]):
            match = tab[info + CODES[e]] == tab[T_NAME + g * SLOTS + 4 + e]
            terms[4 + e].append((4 + d, match, base + 1 + j))
    return terms


def no_terms():
    return {o: [] for o in range(OWN, SLOTS)}


def offsets(dirs):
    out, total = {}, 0
    for d in dirs:
        out[d] = total
        total += 2 * (COUNT[d] - 1)
    return out, total


EARLY = (0, 1, 2, 5, 7)
PAIR = (6,)
LATE = (3, 4)
EARLY_AT, N_EARLY = offsets(EARLY)
PAIR_AT, N_PAIR = offsets(PAIR)
LATE_AT, N_LATE = offsets(LATE)


def widen(ref, start, out, at, count):
    def one(i, _):
        out[at + i] = split(ref[start + i])
        return 0

    lax.fori_loop(0, count, one, 0, unroll=2)


def chain(total, listed, lefts, rights, zeros):
    for left, match, index in listed:
        total = add(total, product(masked(match, lefts(left), zeros), rights[index]))
    return total


def early_kernel(tab, wide, square_in, near_m, near_p, far_m, far_p, beside, after, also,
                 own, early, square, back_buf, zeros):
    del after, also
    zeros[...] = jnp.zeros_like(zeros)
    for d, ref in ((0, far_m), (1, beside), (2, far_p), (5, near_m), (7, near_p)):
        for k in range(2):
            own[2 * d + k] = split(ref[k])
        widen(ref, 2, early, EARLY_AT[d], 2 * (COUNT[d] - 1))

    def rows(g, _):
        back = own_terms(tab, g, EARLY)
        terms = far_terms(tab, g, EARLY, EARLY_AT, no_terms())
        lefts = lambda left: wide[g * SLOTS + left]
        for i, (left, number, index) in enumerate(back):
            back_buf[i] = halves(product(lefts(left), own[index]))
        for o in range(SLOTS):
            value = square_in[g * SLOTS + o]
            if o >= OWN and terms[o]:
                value = value + halves(chain(None, terms[o], lefts, early, zeros))
            square[g * SLOTS + o] = value
        for i, (left, number, index) in enumerate(back):
            square[g * SLOTS + number] = square[g * SLOTS + number] + back_buf[i]
        return 0

    lax.fori_loop(0, OWN, rows, 0)


def pair_kernel(tab, wide, square_in, pair_in, own, pair, square, cube, back_buf, wsq, zeros):
    zeros[...] = jnp.zeros_like(zeros)
    for d, start in ((6, 0), (3, 12), (4, 14)):
        for k in range(2):
            own[2 * d + k] = split(pair_in[start + k])
    widen(pair_in, 2, pair, 0, N_PAIR)

    def rows(g, _):
        back = own_terms(tab, g, PAIR + LATE)
        terms = far_terms(tab, g, PAIR, PAIR_AT, no_terms())
        lefts = lambda left: wide[g * SLOTS + left]
        for i, (left, number, index) in enumerate(back):
            back_buf[i] = halves(product(lefts(left), own[index]))
        for o in range(SLOTS):
            value = square_in[g * SLOTS + o]
            if o >= OWN and terms[o]:
                value = value + halves(chain(None, terms[o], lefts, pair, zeros))
            square[g * SLOTS + o] = value
        for i, (left, number, index) in enumerate(back):
            square[g * SLOTS + number] = square[g * SLOTS + number] + back_buf[i]
        for o in range(OWN):
            wsq[o] = split(square[g * SLOTS + o])
        for o in range(SLOTS):
            total = None
            for s in range(OWN):
                left = wsq[s]
                if o >= OWN:
                    left = masked(same_name(tab, g, s, o), left, zeros)
                total = add(total, product(left, wide[s * SLOTS + o]))
            cube[g * SLOTS + o] = halves(total)
        return 0

    lax.fori_loop(0, OWN, rows, 0)


def final_kernel(tab, wide, own_early, own_late, early, pair, square, cube, behind, ahead, ham,
                 purified, virial, late, far_square, wsq, own_cube, out_buf, sums, zeros, out_sem):
    zeros[...] = jnp.zeros_like(zeros)
    sums[...] = jnp.zeros_like(sums)
    for d, ref in ((3, behind), (4, ahead)):
        widen(ref, 0, late, LATE_AT[d], 10)

    def rows(g, _):
        late_terms = far_terms(tab, g, LATE, LATE_AT, no_terms())
        pair_terms = far_terms(tab, g, PAIR, PAIR_AT, no_terms())
        early_terms = far_terms(tab, g, EARLY, EARLY_AT, no_terms())
        lefts = lambda left: wide[g * SLOTS + left]
        for o in range(OWN, SLOTS):
            total = chain(None, late_terms[o], lefts, late, zeros)
            value = square[g * SLOTS + o] + halves(total)
            far_square[o - OWN] = value
            wsq[o - OWN] = split(value)

        def finish(o, value):
            slot = tab[T_SLOT + g * SLOTS + o]
            out_buf[g, slot] = value
            for c in range(9):
                part = ham[c, g, slot].astype(jnp.float32) * value
                sums[c] += jnp.sum(part.reshape(EDGE // 8, 8, EDGE), axis=0)

        lefts = lambda left: wsq[left - OWN]
        for o in range(OWN):
            own_cube[o] = cube[g * SLOTS + o]
        for dirs, own in ((EARLY, own_early), (PAIR + LATE, own_late)):
            for left, number, index in own_terms(tab, g, dirs):
                term = halves(product(lefts(left), own[index]))
                own_cube[number] = own_cube[number] + term
        for o in range(OWN, SLOTS):
            total = chain(None, pair_terms[o], lefts, pair, zeros)
            total = chain(total, early_terms[o], lefts, early, zeros)
            total = chain(total, late_terms[o], lefts, late, zeros)
            finish(o, 3.0 * far_square[o - OWN] - 2.0 * (cube[g * SLOTS + o] + halves(total)))
        for o in range(OWN):
            finish(o, 3.0 * square[g * SLOTS + o] - 2.0 * own_cube[o])
        pltpu.make_async_copy(out_buf.at[g], purified.at[g], out_sem.at[g]).start()
        return 0

    lax.fori_loop(0, OWN, rows, 0)
    lane = lax.broadcasted_iota(jnp.int32, (8, EDGE), 1)
    line = jnp.zeros((8, EDGE), jnp.float32)
    for c in range(9):
        line = jnp.where(lane == c, jnp.sum(sums[c]), line)
    for i in range(N_DEV // 8):
        virial[pl.ds(i * 8, 8)] = line
    for g in range(OWN):
        pltpu.make_async_copy(out_buf.at[g], purified.at[g], out_sem.at[g]).wait()


def from_direction(d):
    dr, dc = DIRS[d]
    pairs = []
    for row in range(N_ROW):
        for col in range(N_COL):
            towards = 1 - 2 * (row & 1)
            there = (row + dr * towards) % N_ROW * N_COL + (col + dc) % N_COL
            pairs.append((there, row * N_COL + col))
    return pairs


ANY = pl.BlockSpec(memory_space=pl.ANY)
VMEM = pl.BlockSpec(memory_space=pltpu.VMEM)
SMEM = pl.BlockSpec(memory_space=pltpu.SMEM)
HBM = pl.BlockSpec(memory_space=pltpu.HBM)
F32 = jnp.float32
BF16 = jnp.bfloat16


def call(kernel, name, out, in_specs, out_specs, scratch, flops, moved, vmem=32):
    return pl.pallas_call(
        kernel,
        out_shape=out,
        in_specs=in_specs,
        out_specs=out_specs,
        scratch_shapes=scratch,
        compiler_params=pltpu.CompilerParams(vmem_limit_bytes=vmem << 20),
        cost_estimate=pl.CostEstimate(
            flops=flops * 2 * 4 * EDGE**3, bytes_accessed=moved << 20, transcendentals=0
        ),
        name=name,
    )


def blocks(*lead):
    return jax.ShapeDtypeStruct(lead + (EDGE, EDGE), F32)


def wides(*lead):
    return jax.ShapeDtypeStruct(lead + (EDGE, 2 * EDGE), BF16)


def wide_scratch(*lead):
    return pltpu.VMEM(lead + (EDGE, 2 * EDGE), BF16)


def scratch(*lead):
    return pltpu.VMEM(lead + (EDGE, EDGE), F32)


def body(density, pattern, ham_strain):
    dma = pltpu.SemaphoreType.DMA
    table = jax.ShapeDtypeStruct((T_SIZE,), jnp.int32)
    dens, tab, near_m, near_p, far_m, far_p, beside = call(
        first_kernel, "first",
        (blocks(OWN * SLOTS), table, blocks(10), blocks(10), blocks(8), blocks(8), blocks(12)),
        [HBM, HBM], (VMEM, SMEM) + (VMEM,) * 5,
        [pltpu.SMEM((SLOTS, N_DEV * OWN), jnp.int32), dma((2,))], 0, 10, 53,
    )(pattern.T, density.reshape(OWN * SLOTS, EDGE, EDGE))
    near_ahead = lax.ppermute(near_m, AXES, from_direction(7))
    near_behind = lax.ppermute(near_p, AXES, from_direction(5))
    far_ahead = lax.ppermute(far_m, AXES, from_direction(2))
    far_behind = lax.ppermute(far_p, AXES, from_direction(0))
    beside = lax.ppermute(beside, AXES, from_direction(1))
    tab, wide, square, ham = call(
        local_kernel, "local",
        (table, wides(OWN * SLOTS), blocks(OWN * SLOTS),
         jax.ShapeDtypeStruct(ham_strain.shape, BF16)),
        [SMEM, VMEM, SMEM, HBM], (SMEM, VMEM, VMEM, VMEM), [wide_scratch(), dma((9,))], 192, 36,
    )(pattern.T, dens, tab, ham_strain)
    pair, late_m, late_p = call(
        second_kernel, "second", (blocks(16), blocks(10), blocks(10)),
        [SMEM] + [VMEM] * 3 + [ANY] * 4, (VMEM,) * 3, [], 0, 4,
    )(tab, dens, near_behind, near_ahead, far_behind, far_ahead, beside, square)
    late_ahead = lax.ppermute(late_m, AXES, from_direction(4))
    late_behind = lax.ppermute(late_p, AXES, from_direction(3))
    pair_in = lax.ppermute(pair, AXES, from_direction(6))
    own_early, early, square = call(
        early_kernel, "early",
        (wides(16), wides(N_EARLY), blocks(OWN * SLOTS)),
        [SMEM] + [VMEM] * 7 + [ANY] * 2, (VMEM,) * 3,
        [scratch(8), wide_scratch()], 88, 10,
    )(tab, wide, square, near_behind, near_ahead, far_behind, far_ahead, beside, pair, late_m)
    own_late, pair, square, cube = call(
        pair_kernel, "pair",
        (wides(16), wides(N_PAIR), blocks(OWN * SLOTS), blocks(OWN * SLOTS)),
        [SMEM] + [VMEM] * 3, (VMEM,) * 4,
        [scratch(8), wide_scratch(OWN), wide_scratch()], 224, 10,
    )(tab, wide, square, pair_in)
    purified, line = call(
        final_kernel, "final",
        (blocks(OWN, SLOTS), jax.ShapeDtypeStruct((N_DEV, EDGE), F32)),
        [SMEM] + [VMEM] * 10, (ANY, VMEM),
        [
            wide_scratch(N_LATE), scratch(8), wide_scratch(8), scratch(OWN),
            scratch(OWN, SLOTS), pltpu.VMEM((9, 8, EDGE), F32), wide_scratch(), dma((OWN,)),
        ], 200, 30,
    )(tab, wide, own_early, own_late, early, pair, square, cube, late_behind, late_ahead, ham)
    total_blocks = N_DEV * OWN
    factor = 1.0 / math.sqrt(float(total_blocks * SLOTS * EDGE * EDGE))
    lines = lax.all_to_all(line, AXES, 0, 0, tiled=True)
    virial = (jnp.sum(lines, axis=0)[:9] * factor).reshape(3, 3)
    return purified, virial


def solution(mesh):
    in_specs = (P(AXES, None, None, None), P(), P(None, AXES, None, None, None))
    out_specs = (P(AXES, None, None, None), P())
    return jax.shard_map(body, mesh=mesh, in_specs=in_specs, out_specs=out_specs, check_vma=False)
```

```python
import math

import jax
import jax.numpy as jnp
from jax import lax
from jax.experimental import pallas as pl
from jax.experimental.pallas import tpu as pltpu
from jax.sharding import PartitionSpec as P

AXES = ("row", "col")
EDGE = 128
OWN = 4
SLOTS = 12
N_ROW = 16
N_COL = 8
N_DEV = N_ROW * N_COL

DIRS = ((-1, -1), (-1, 0), (-1, 1), (0, -1), (0, 1), (1, -1), (1, 0), (1, 1))


def near(a, b):
    return max(abs(a[0] - b[0]), abs(a[1] - b[1])) <= 1


COMMON = tuple(
    tuple(e for e in range(8) if e != d and near(DIRS[e], DIRS[d])) for d in range(8)
)
COUNT = tuple(2 + len(COMMON[d]) for d in range(8))
BACK = tuple(DIRS.index((dr, -dc)) for dr, dc in DIRS)
SEEN = tuple(
    tuple(
        DIRS.index(
            (
                (DIRS[e][0] - DIRS[d][0]) * (1 if DIRS[d][0] == 0 else -1),
                DIRS[e][1] - DIRS[d][1],
            )
        )
        for e in COMMON[d]
    )
    for d in range(8)
)

T_SLOT = 0
T_NAME = 48
T_LOW = 96
T_FAR = 104
T_SEND = 264
T_SIZE = 264 + 80
SEND_AT = tuple(T_SEND + 2 * sum(COUNT[:f]) for f in range(8))
CODES = tuple((dr + 1) * 3 + dc + 1 for dr, dc in DIRS)


def place(value, row, col):
    dev = value >> 2
    dr = ((dev >> 3) - row + 1) & (N_ROW - 1)
    dc = ((dev & (N_COL - 1)) - col + 1) & (N_COL - 1)
    return jnp.where(((row & 1) == 1) & (dr < 3), 2 - dr, dr), dc


def device_at(row, col, d):
    dr, dc = DIRS[d]
    towards = 1 - 2 * (row & 1)
    return ((row + dr * towards) & (N_ROW - 1)) * N_COL + ((col + dc) & (N_COL - 1))


def own_table(pat, row, col, tab):
    me = row * N_COL + col
    for l in range(OWN):
        for u in range(SLOTS):
            value = pat[u, me * OWN + l]
            dr, dc = place(value, row, col)
            code = dr * 3 + dc
            number = value & 3
            o = jnp.where(code == 4, number, code + jnp.where(code > 4, 3, 4))
            tab[T_SLOT + l * SLOTS + o] = u
            tab[T_NAME + l * SLOTS + o] = number


def named_rows(pat, other, me):
    named = []
    for j in range(OWN):
        number = jnp.int32(0)
        for u in range(SLOTS):
            value = pat[u, other * OWN + j]
            number = jnp.where((value >> 2) == me, value & 3, number)
        named.append(number)
    low = jnp.minimum(jnp.minimum(named[0], named[1]), jnp.minimum(named[2], named[3]))
    high = jnp.maximum(jnp.maximum(named[0], named[1]), jnp.maximum(named[2], named[3]))
    return low, high


def send_table(pat, row, col, tab):
    for f in range(8):
        d = BACK[f]
        rows = named_rows(pat, device_at(row, col, f), row * N_COL + col)
        for k, l in enumerate(rows):
            columns = [l, 4 + f] + [4 + e for e in SEEN[d]]
            for m, o in enumerate(columns):
                tab[SEND_AT[f] + k * COUNT[d] + m] = l * SLOTS + tab[T_SLOT + l * SLOTS + o]


def own_of(tab, f, k):
    return tab[SEND_AT[f] + k * COUNT[f] + 1]


def rest_of(tab, f, k):
    at = SEND_AT[f] + k * COUNT[f]
    return [tab[at]] + [tab[at + m] for m in range(2, COUNT[f])]


def fill(out, tab, dens, f, low=0, high=12):
    numbers = [own_of(tab, f, k) for k in range(2)] + rest_of(tab, f, 0) + rest_of(tab, f, 1)
    for i, n in enumerate(numbers[low:high]):
        out[i] = dens[n]


def first_kernel(pat_in, dens_in, tab, near_m, near_p, far_m, far_p, beside, dens, pat, sem):
    load = pltpu.make_async_copy(dens_in, dens, sem.at[0])
    load.start()
    pat_load = pltpu.make_async_copy(pat_in, pat, sem.at[1])
    pat_load.start()
    pat_load.wait()
    row = lax.axis_index("row")
    col = lax.axis_index("col")
    own_table(pat, row, col, tab)
    send_table(pat, row, col, tab)
    load.wait()
    for out, f, edge in ((near_m, 5, 3), (near_p, 7, 4)):
        fill(out, tab, dens, f)
        for k in range(2):
            out[8 + k] = dens[own_of(tab, edge, k)]
    for out, f in ((far_m, 0), (far_p, 2)):
        fill(out, tab, dens, f)
    fill(beside, tab, dens, 1, 0, 2)


def second_kernel(tab, dens, behind, ahead, *refs):
    late_m, late_p, beside, pair_low, pair_high = refs[1:]
    fill(pair_low, tab, dens, 6, 0, 8)
    fill(pair_high, tab, dens, 6, 8, 12)
    for k in range(2):
        pair_high[4 + k] = behind[8 + k]
        pair_high[6 + k] = ahead[8 + k]
    for f, out in ((3, late_m), (4, late_p), (1, beside)):
        fill(out, tab, dens, f, 2, 12)


def far_table(pat, row, col, tab):
    for d in range(8):
        names = [tab[T_NAME + l * SLOTS + 4 + d] for l in range(OWN)]
        low = jnp.minimum(jnp.minimum(names[0], names[1]), jnp.minimum(names[2], names[3]))
        high = jnp.maximum(jnp.maximum(names[0], names[1]), jnp.maximum(names[2], names[3]))
        tab[T_LOW + d] = low
        other = device_at(row, col, d)
        for k, l in enumerate((low, high)):
            for u in range(SLOTS):
                value = pat[u, other * OWN + l]
                dr, dc = place(value, row, col)
                code = jnp.where((dr < 3) & (dc < 3), dr * 3 + dc, 9)
                tab[T_FAR + (2 * d + k) * 10 + code] = value & 3


def split(value):
    high = value.astype(jnp.bfloat16)
    low = (value - high.astype(jnp.float32)).astype(jnp.bfloat16)
    return jnp.concatenate([high, low], axis=1)


def product(left, right):
    return jnp.dot(
        left, jnp.concatenate([right, right], axis=0), preferred_element_type=jnp.float32
    )


def halves(value):
    return value[:, :EDGE] + value[:, EDGE:]


def bit(tab, g, d):
    return jnp.where(tab[T_NAME + g * SLOTS + 4 + d] == tab[T_LOW + d], 0, 1)


def local_kernel(pat, dens, tab_in, after, tab, wide, square, zeros):
    del after
    row = lax.axis_index("row")
    col = lax.axis_index("col")
    for i in range(T_LOW):
        tab[i] = tab_in[i]
    for i in range(T_SEND, T_SIZE):
        tab[i] = tab_in[i]
    far_table(pat, row, col, tab)
    zeros[...] = jnp.zeros_like(zeros)

    def widen(i, _):
        wide[i] = split(dens[i // SLOTS * SLOTS + tab[T_SLOT + i]])
        return 0

    lax.fori_loop(0, OWN * SLOTS, widen, 0)

    def rows(g, _):
        for t in range(SLOTS):
            total = None
            for s in range(OWN):
                left = wide[g * SLOTS + s]
                if t >= OWN:
                    left = masked(same_name(tab, g, s, t), left, zeros)
                total = add(total, product(left, wide[s * SLOTS + t]))
            square[g * SLOTS + t] = halves(total)
        return 0

    lax.fori_loop(0, OWN, rows, 0)


def masked(match, left, zeros):
    if match is None:
        return left
    return jnp.where(match, left, zeros[...])


def same_name(tab, g, s, o):
    return bit(tab, g, o - OWN) == bit(tab, s, o - OWN)


def add(total, term):
    return term if total is None else total + term


def own_terms(tab, g, dirs):
    out = []
    for d in dirs:
        b = bit(tab, g, d)
        out.append((4 + d, tab[T_FAR + (2 * d + b) * 10 + 4], 2 * d + b))
    return out


def far_terms(tab, g, dirs, at, terms):
    for d in dirs:
        b = bit(tab, g, d)
        base = at[d] + b * (COUNT[d] - 1)
        info = T_FAR + (2 * d + b) * 10
        terms[4 + d].append((4 + d, None, base))
        for j, e in enumerate(COMMON[d]):
            match = tab[info + CODES[e]] == tab[T_NAME + g * SLOTS + 4 + e]
            terms[4 + e].append((4 + d, match, base + 1 + j))
    return terms


def no_terms():
    return {o: [] for o in range(OWN, SLOTS)}


def offsets(dirs):
    out, total = {}, 0
    for d in dirs:
        out[d] = total
        total += 2 * (COUNT[d] - 1)
    return out, total


EARLY = (0, 2, 5, 7)
PAIR = (6,)
LATE = (3, 4, 1)
EARLY_AT, N_EARLY = offsets(EARLY)
PAIR_AT, N_PAIR = offsets(PAIR)
LATE_AT, N_LATE = offsets(LATE)


def widen(ref, start, out, at, count):
    def one(i, _):
        out[at + i] = split(ref[start + i])
        return 0

    lax.fori_loop(0, count, one, 0, unroll=2)


def chain(total, listed, lefts, rights, zeros):
    for left, match, index in listed:
        total = add(total, product(masked(match, lefts(left), zeros), rights[index]))
    return total


def early_kernel(tab, wide, square_in, near_m, near_p, far_m, far_p, after, also,
                 own, early, square, back_buf, zeros):
    del after, also
    zeros[...] = jnp.zeros_like(zeros)
    for d, ref in ((0, far_m), (2, far_p), (5, near_m), (7, near_p)):
        for k in range(2):
            own[2 * d + k] = split(ref[k])
        widen(ref, 2, early, EARLY_AT[d], 2 * (COUNT[d] - 1))

    def rows(g, _):
        back = own_terms(tab, g, EARLY)
        terms = far_terms(tab, g, EARLY, EARLY_AT, no_terms())
        lefts = lambda left: wide[g * SLOTS + left]
        for i, (left, number, index) in enumerate(back):
            back_buf[i] = halves(product(lefts(left), own[index]))
        for o in range(SLOTS):
            value = square_in[g * SLOTS + o]
            if o >= OWN and terms[o]:
                value = value + halves(chain(None, terms[o], lefts, early, zeros))
            square[g * SLOTS + o] = value
        for i, (left, number, index) in enumerate(back):
            square[g * SLOTS + number] = square[g * SLOTS + number] + back_buf[i]
        return 0

    lax.fori_loop(0, OWN, rows, 0)


def pair_kernel(tab, wide, square_in, low, high, beside,
                own, pair, square, cube, back_buf, wsq, zeros):
    zeros[...] = jnp.zeros_like(zeros)
    for d, ref, start in ((6, low, 0), (1, beside, 0), (3, high, 4), (4, high, 6)):
        for k in range(2):
            own[2 * d + k] = split(ref[start + k])
    widen(low, 2, pair, 0, 6)
    widen(high, 0, pair, 6, 4)

    def rows(g, _):
        back = own_terms(tab, g, PAIR + LATE)
        terms = far_terms(tab, g, PAIR, PAIR_AT, no_terms())
        lefts = lambda left: wide[g * SLOTS + left]
        for i, (left, number, index) in enumerate(back):
            back_buf[i] = halves(product(lefts(left), own[index]))
        for o in range(SLOTS):
            value = square_in[g * SLOTS + o]
            if o >= OWN and terms[o]:
                value = value + halves(chain(None, terms[o], lefts, pair, zeros))
            square[g * SLOTS + o] = value
        for i, (left, number, index) in enumerate(back):
            square[g * SLOTS + number] = square[g * SLOTS + number] + back_buf[i]
        for o in range(OWN):
            wsq[o] = split(square[g * SLOTS + o])
        for o in range(SLOTS):
            total = None
            for s in range(OWN):
                left = wsq[s]
                if o >= OWN:
                    left = masked(same_name(tab, g, s, o), left, zeros)
                total = add(total, product(left, wide[s * SLOTS + o]))
            cube[g * SLOTS + o] = halves(total)
        return 0

    lax.fori_loop(0, OWN, rows, 0)


def final_kernel(tab, wide, own_early, own_late, early, pair, square, cube, behind, ahead, beside, ham,
                 purified, virial, late, far_square, wsq, own_cube, back_buf, out_buf, sums, zeros, out_sem):
    zeros[...] = jnp.zeros_like(zeros)
    sums[...] = jnp.zeros_like(sums)
    for d, ref in ((3, behind), (4, ahead), (1, beside)):
        widen(ref, 0, late, LATE_AT[d], 10)

    def squares(g, _):
        terms = far_terms(tab, g, LATE, LATE_AT, no_terms())
        lefts = lambda left: wide[g * SLOTS + left]
        sums_of = [halves(chain(None, terms[o], lefts, late, zeros)) for o in range(OWN, SLOTS)]
        for i, total in enumerate(sums_of):
            value = square[g * SLOTS + OWN + i] + total
            far_square[g * 8 + i] = value
            wsq[g * 8 + i] = split(value)
        return 0

    lax.fori_loop(0, OWN, squares, 0, unroll=4)

    def rows(g, _):
        terms = far_terms(tab, g, PAIR, PAIR_AT, no_terms())
        early_terms = far_terms(tab, g, EARLY, EARLY_AT, no_terms())
        late_terms = far_terms(tab, g, LATE, LATE_AT, no_terms())
        lefts = lambda left: wsq[g * 8 + left - OWN]

        def finish(o, value):
            slot = tab[T_SLOT + g * SLOTS + o]
            out_buf[g, slot] = value
            for c in range(9):
                part = ham[c, g, slot].astype(jnp.float32) * value
                sums[c] += jnp.sum(part.reshape(EDGE // 8, 8, EDGE), axis=0)

        back = own_terms(tab, g, EARLY) + own_terms(tab, g, PAIR + LATE)
        backs = []
        for i, (left, number, index) in enumerate(back):
            own = own_early if i < len(EARLY) else own_late
            backs.append(halves(product(lefts(left), own[index])))
        cubes = []
        for o in range(OWN, SLOTS):
            if len(cubes) == 0:
                for i, total in enumerate(backs):
                    back_buf[i] = total
            total = chain(None, terms[o], lefts, pair, zeros)
            total = chain(total, early_terms[o], lefts, early, zeros)
            total = chain(total, late_terms[o], lefts, late, zeros)
            cubes.append(halves(total))
        for i, total in enumerate(cubes):
            o = OWN + i
            value = cube[g * SLOTS + o] + total
            finish(o, 3.0 * far_square[g * 8 + i] - 2.0 * value)
        for o in range(OWN):
            own_cube[o] = 3.0 * square[g * SLOTS + o] - 2.0 * cube[g * SLOTS + o]
        for i, (left, number, index) in enumerate(back):
            own_cube[number] = own_cube[number] - 2.0 * back_buf[i]
        for o in range(OWN):
            finish(o, own_cube[o])
        pltpu.make_async_copy(out_buf.at[g], purified.at[g], out_sem.at[g]).start()
        return 0

    lax.fori_loop(0, OWN, rows, 0, unroll=2)
    lane = lax.broadcasted_iota(jnp.int32, (8, EDGE), 1)
    line = jnp.zeros((8, EDGE), jnp.float32)
    for c in range(9):
        line = jnp.where(lane == c, jnp.sum(sums[c]), line)
    for i in range(N_DEV // 8):
        virial[pl.ds(i * 8, 8)] = line
    for g in range(OWN):
        pltpu.make_async_copy(out_buf.at[g], purified.at[g], out_sem.at[g]).wait()


def from_direction(d):
    dr, dc = DIRS[d]
    pairs = []
    for row in range(N_ROW):
        for col in range(N_COL):
            towards = 1 - 2 * (row & 1)
            there = (row + dr * towards) % N_ROW * N_COL + (col + dc) % N_COL
            pairs.append((there, row * N_COL + col))
    return pairs


ANY = pl.BlockSpec(memory_space=pl.ANY)
VMEM = pl.BlockSpec(memory_space=pltpu.VMEM)
SMEM = pl.BlockSpec(memory_space=pltpu.SMEM)
HBM = pl.BlockSpec(memory_space=pltpu.HBM)
F32 = jnp.float32
BF16 = jnp.bfloat16


def call(kernel, name, out, in_specs, out_specs, scratch, flops, moved, vmem=12):
    return pl.pallas_call(
        kernel,
        out_shape=out,
        in_specs=in_specs,
        out_specs=out_specs,
        scratch_shapes=scratch,
        compiler_params=pltpu.CompilerParams(vmem_limit_bytes=vmem << 20),
        cost_estimate=pl.CostEstimate(
            flops=flops * 2 * 4 * EDGE**3, bytes_accessed=moved << 20, transcendentals=0
        ),
        name=name,
    )


def blocks(*lead):
    return jax.ShapeDtypeStruct(lead + (EDGE, EDGE), F32)


def wides(*lead):
    return jax.ShapeDtypeStruct(lead + (EDGE, 2 * EDGE), BF16)


def wide_scratch(*lead):
    return pltpu.VMEM(lead + (EDGE, 2 * EDGE), BF16)


def scratch(*lead):
    return pltpu.VMEM(lead + (EDGE, EDGE), F32)


def body(density, pattern, ham_strain):
    dma = pltpu.SemaphoreType.DMA
    table = jax.ShapeDtypeStruct((T_SIZE,), jnp.int32)
    dens = density.reshape(OWN * SLOTS, EDGE, EDGE)
    tab, near_m, near_p, far_m, far_p, beside_own = call(
        first_kernel, "first", (table, blocks(10), blocks(10), blocks(8), blocks(8), blocks(2)),
        [HBM, HBM], (SMEM,) + (VMEM,) * 5,
        [scratch(OWN * SLOTS), pltpu.SMEM((SLOTS, N_DEV * OWN), jnp.int32), dma((2,))], 0, 10, 56,
    )(pattern.T, dens)
    near_ahead = lax.ppermute(near_m, AXES, from_direction(7))
    near_behind = lax.ppermute(near_p, AXES, from_direction(5))
    far_ahead = lax.ppermute(far_m, AXES, from_direction(2))
    far_behind = lax.ppermute(far_p, AXES, from_direction(0))
    beside_own = lax.ppermute(beside_own, AXES, from_direction(1))
    tab, wide, square = call(
        local_kernel, "local",
        (table, wides(OWN * SLOTS), blocks(OWN * SLOTS)),
        [SMEM, VMEM, SMEM, ANY], (SMEM,) + (VMEM,) * 2, [wide_scratch()], 400, 9,
    )(pattern.T, dens, tab, beside_own)
    late_m, late_p, beside, pair_low, pair_high = call(
        second_kernel, "second", (blocks(10), blocks(10), blocks(10), blocks(8), blocks(8)),
        [SMEM] + [VMEM] * 3 + [ANY], (VMEM,) * 5, [], 0, 5,
    )(tab, dens, near_behind, near_ahead, square)
    late_ahead = lax.ppermute(late_m, AXES, from_direction(4))
    late_behind = lax.ppermute(late_p, AXES, from_direction(3))
    pair_low_in = lax.ppermute(pair_low, AXES, from_direction(6))
    pair_high_in = lax.ppermute(pair_high, AXES, from_direction(6))
    beside_in = lax.ppermute(beside, AXES, from_direction(1))
    own_early, early, square = call(
        early_kernel, "early",
        (wides(16), wides(N_EARLY), blocks(OWN * SLOTS)),
        [SMEM] + [VMEM] * 6 + [ANY] * 2, (VMEM,) * 3,
        [scratch(8), wide_scratch()], 0, 0,
    )(tab, wide, square, near_behind, near_ahead, far_behind, far_ahead, beside, late_m)
    own_late, pair, square, cube = call(
        pair_kernel, "pair",
        (wides(16), wides(N_PAIR), blocks(OWN * SLOTS), blocks(OWN * SLOTS)),
        [SMEM] + [VMEM] * 5, (VMEM,) * 4,
        [scratch(8), wide_scratch(OWN), wide_scratch()], 0, 0,
    )(tab, wide, square, pair_low_in, pair_high_in, beside_own)
    purified, line = call(
        final_kernel, "final",
        (blocks(OWN, SLOTS), jax.ShapeDtypeStruct((N_DEV, EDGE), F32)),
        [SMEM] + [VMEM] * 11, (ANY, VMEM),
        [
            wide_scratch(N_LATE), scratch(8 * OWN), wide_scratch(8 * OWN), scratch(OWN), scratch(8),
            scratch(OWN, SLOTS), pltpu.VMEM((9, 8, EDGE), F32), wide_scratch(), dma((OWN,)),
        ], 200, 30,
    )(tab, wide, own_early, own_late, early, pair, square, cube, late_behind, late_ahead, beside_in,
      ham_strain)
    total_blocks = N_DEV * OWN
    factor = 1.0 / math.sqrt(float(total_blocks * SLOTS * EDGE * EDGE))
    lines = lax.all_to_all(line, AXES, 0, 0, tiled=True)
    virial = (jnp.sum(lines, axis=0)[:9] * factor).reshape(3, 3)
    return purified, virial


def solution(mesh):
    in_specs = (P(AXES, None, None, None), P(), P(None, AXES, None, None, None))
    out_specs = (P(AXES, None, None, None), P())
    return jax.shard_map(body, mesh=mesh, in_specs=in_specs, out_specs=out_specs, check_vma=False)
```

```python
import math

import jax
import jax.numpy as jnp
from jax import lax
from jax.experimental import pallas as pl
from jax.experimental.pallas import tpu as pltpu
from jax.sharding import PartitionSpec as P

AXES = ("row", "col")
EDGE = 128
OWN = 4
SLOTS = 12
N_ROW = 16
N_COL = 8
N_DEV = N_ROW * N_COL

DIRS = ((-1, -1), (-1, 0), (-1, 1), (0, -1), (0, 1), (1, -1), (1, 0), (1, 1))


def near(a, b):
    return max(abs(a[0] - b[0]), abs(a[1] - b[1])) <= 1


COMMON = tuple(
    tuple(e for e in range(8) if e != d and near(DIRS[e], DIRS[d])) for d in range(8)
)
COUNT = tuple(2 + len(COMMON[d]) for d in range(8))
BACK = tuple(DIRS.index((dr, -dc)) for dr, dc in DIRS)
SEEN = tuple(
    tuple(
        DIRS.index(
            (
                (DIRS[e][0] - DIRS[d][0]) * (1 if DIRS[d][0] == 0 else -1),
                DIRS[e][1] - DIRS[d][1],
            )
        )
        for e in COMMON[d]
    )
    for d in range(8)
)

T_SLOT = 0
T_NAME = 48
T_LOW = 96
T_FAR = 104
T_SEND = 264
T_SIZE = 264 + 80
SEND_AT = tuple(T_SEND + 2 * sum(COUNT[:f]) for f in range(8))
CODES = tuple((dr + 1) * 3 + dc + 1 for dr, dc in DIRS)


def place(value, row, col):
    dev = value >> 2
    dr = ((dev >> 3) - row + 1) & (N_ROW - 1)
    dc = ((dev & (N_COL - 1)) - col + 1) & (N_COL - 1)
    return jnp.where(((row & 1) == 1) & (dr < 3), 2 - dr, dr), dc


def device_at(row, col, d):
    dr, dc = DIRS[d]
    towards = 1 - 2 * (row & 1)
    return ((row + dr * towards) & (N_ROW - 1)) * N_COL + ((col + dc) & (N_COL - 1))


def own_table(pat, row, col, tab):
    me = row * N_COL + col
    for l in range(OWN):
        for u in range(SLOTS):
            value = pat[u, me * OWN + l]
            dr, dc = place(value, row, col)
            code = dr * 3 + dc
            number = value & 3
            o = jnp.where(code == 4, number, code + jnp.where(code > 4, 3, 4))
            tab[T_SLOT + l * SLOTS + o] = u
            tab[T_NAME + l * SLOTS + o] = number


def named_rows(pat, other, me):
    named = []
    for j in range(OWN):
        number = jnp.int32(0)
        for u in range(SLOTS):
            value = pat[u, other * OWN + j]
            number = jnp.where((value >> 2) == me, value & 3, number)
        named.append(number)
    low = jnp.minimum(jnp.minimum(named[0], named[1]), jnp.minimum(named[2], named[3]))
    high = jnp.maximum(jnp.maximum(named[0], named[1]), jnp.maximum(named[2], named[3]))
    return low, high


def send_table(pat, row, col, tab):
    for f in range(8):
        d = BACK[f]
        rows = named_rows(pat, device_at(row, col, f), row * N_COL + col)
        for k, l in enumerate(rows):
            columns = [l, 4 + f] + [4 + e for e in SEEN[d]]
            for m, o in enumerate(columns):
                tab[SEND_AT[f] + k * COUNT[d] + m] = l * SLOTS + tab[T_SLOT + l * SLOTS + o]


def own_of(tab, f, k):
    return tab[SEND_AT[f] + k * COUNT[f] + 1]


def rest_of(tab, f, k):
    at = SEND_AT[f] + k * COUNT[f]
    return [tab[at]] + [tab[at + m] for m in range(2, COUNT[f])]


def fill(out, tab, dens, f, low=0, high=12):
    numbers = [own_of(tab, f, k) for k in range(2)] + rest_of(tab, f, 0) + rest_of(tab, f, 1)
    for i, n in enumerate(numbers[low:high]):
        out[i] = dens[n]


def first_kernel(pat_in, dens_in, tab, near_m, near_p, far_m, far_p, beside, dens, pat, sem):
    load = pltpu.make_async_copy(dens_in, dens, sem.at[0])
    load.start()
    pat_load = pltpu.make_async_copy(pat_in, pat, sem.at[1])
    pat_load.start()
    pat_load.wait()
    row = lax.axis_index("row")
    col = lax.axis_index("col")
    own_table(pat, row, col, tab)
    send_table(pat, row, col, tab)
    load.wait()
    for out, f, edge in ((near_m, 5, 3), (near_p, 7, 4)):
        fill(out, tab, dens, f)
        for k in range(2):
            out[8 + k] = dens[own_of(tab, edge, k)]
    for out, f in ((far_m, 0), (far_p, 2)):
        fill(out, tab, dens, f)
    fill(beside, tab, dens, 1, 0, 2)


def late_kernel(tab, dens, *refs):
    for f, out in zip((3, 4, 1), refs[1:]):
        fill(out, tab, dens, f, 2, 12)


def second_kernel(tab, dens, behind, ahead, *refs):
    pair_low, pair_high = refs
    fill(pair_low, tab, dens, 6, 0, 8)
    fill(pair_high, tab, dens, 6, 8, 12)
    for k in range(2):
        pair_high[4 + k] = behind[8 + k]
        pair_high[6 + k] = ahead[8 + k]


def far_table(pat, row, col, tab):
    for d in range(8):
        names = [tab[T_NAME + l * SLOTS + 4 + d] for l in range(OWN)]
        low = jnp.minimum(jnp.minimum(names[0], names[1]), jnp.minimum(names[2], names[3]))
        high = jnp.maximum(jnp.maximum(names[0], names[1]), jnp.maximum(names[2], names[3]))
        tab[T_LOW + d] = low
        other = device_at(row, col, d)
        for k, l in enumerate((low, high)):
            for u in range(SLOTS):
                value = pat[u, other * OWN + l]
                dr, dc = place(value, row, col)
                code = jnp.where((dr < 3) & (dc < 3), dr * 3 + dc, 9)
                tab[T_FAR + (2 * d + k) * 10 + code] = value & 3


def split(value):
    high = value.astype(jnp.bfloat16)
    low = (value - high.astype(jnp.float32)).astype(jnp.bfloat16)
    return jnp.concatenate([high, low], axis=1)


def product(left, right):
    return jnp.dot(
        left, jnp.concatenate([right, right], axis=0), preferred_element_type=jnp.float32
    )


def halves(value):
    return value[:, :EDGE] + value[:, EDGE:]


def bit(tab, g, d):
    return jnp.where(tab[T_NAME + g * SLOTS + 4 + d] == tab[T_LOW + d], 0, 1)


def local_kernel(pat, dens, tab_in, after, tab, wide, square, zeros):
    del after
    row = lax.axis_index("row")
    col = lax.axis_index("col")
    for i in range(T_LOW):
        tab[i] = tab_in[i]
    for i in range(T_SEND, T_SIZE):
        tab[i] = tab_in[i]
    far_table(pat, row, col, tab)
    zeros[...] = jnp.zeros_like(zeros)

    def widen(i, _):
        wide[i] = split(dens[i // SLOTS * SLOTS + tab[T_SLOT + i]])
        return 0

    lax.fori_loop(0, OWN * SLOTS, widen, 0)

    def rows(g, _):
        for t in range(SLOTS):
            total = None
            for s in range(OWN):
                left = wide[g * SLOTS + s]
                if t >= OWN:
                    left = masked(same_name(tab, g, s, t), left, zeros)
                total = add(total, product(left, wide[s * SLOTS + t]))
            square[g * SLOTS + t] = halves(total)
        return 0

    lax.fori_loop(0, OWN, rows, 0)


def masked(match, left, zeros):
    if match is None:
        return left
    return jnp.where(match, left, zeros[...])


def same_name(tab, g, s, o):
    return bit(tab, g, o - OWN) == bit(tab, s, o - OWN)


def add(total, term):
    return term if total is None else total + term


def own_terms(tab, g, dirs):
    out = []
    for d in dirs:
        b = bit(tab, g, d)
        out.append((4 + d, tab[T_FAR + (2 * d + b) * 10 + 4], 2 * d + b))
    return out


def far_terms(tab, g, dirs, at, terms):
    for d in dirs:
        b = bit(tab, g, d)
        base = at[d] + b * (COUNT[d] - 1)
        info = T_FAR + (2 * d + b) * 10
        terms[4 + d].append((4 + d, None, base))
        for j, e in enumerate(COMMON[d]):
            match = tab[info + CODES[e]] == tab[T_NAME + g * SLOTS + 4 + e]
            terms[4 + e].append((4 + d, match, base + 1 + j))
    return terms


def no_terms():
    return {o: [] for o in range(OWN, SLOTS)}


def offsets(dirs):
    out, total = {}, 0
    for d in dirs:
        out[d] = total
        total += 2 * (COUNT[d] - 1)
    return out, total


EARLY = (0, 2, 5, 7)
PAIR = (6,)
LATE = (3, 4, 1)
EARLY_AT, N_EARLY = offsets(EARLY)
PAIR_AT, N_PAIR = offsets(PAIR)
LATE_AT, N_LATE = offsets(LATE)


def widen(ref, start, out, at, count):
    def one(i, _):
        out[at + i] = split(ref[start + i])
        return 0

    lax.fori_loop(0, count, one, 0, unroll=2)


def chain(total, listed, lefts, rights, zeros):
    for left, match, index in listed:
        total = add(total, product(masked(match, lefts(left), zeros), rights[index]))
    return total


def early_kernel(tab, wide, square_in, near_m, near_p, far_m, far_p, after, also,
                 own, early, square, back_buf, zeros):
    del after, also
    zeros[...] = jnp.zeros_like(zeros)
    for d, ref in ((0, far_m), (2, far_p), (5, near_m), (7, near_p)):
        for k in range(2):
            own[2 * d + k] = split(ref[k])
        widen(ref, 2, early, EARLY_AT[d], 2 * (COUNT[d] - 1))

    def rows(g, _):
        back = own_terms(tab, g, EARLY)
        terms = far_terms(tab, g, EARLY, EARLY_AT, no_terms())
        lefts = lambda left: wide[g * SLOTS + left]
        for i, (left, number, index) in enumerate(back):
            back_buf[i] = halves(product(lefts(left), own[index]))
        for o in range(SLOTS):
            value = square_in[g * SLOTS + o]
            if o >= OWN and terms[o]:
                value = value + halves(chain(None, terms[o], lefts, early, zeros))
            square[g * SLOTS + o] = value
        for i, (left, number, index) in enumerate(back):
            square[g * SLOTS + number] = square[g * SLOTS + number] + back_buf[i]
        return 0

    lax.fori_loop(0, OWN, rows, 0)


def pair_kernel(tab, wide, square_in, low, high, beside,
                own, pair, square, cube, back_buf, wsq, zeros):
    zeros[...] = jnp.zeros_like(zeros)
    for d, ref, start in ((6, low, 0), (1, beside, 0), (3, high, 4), (4, high, 6)):
        for k in range(2):
            own[2 * d + k] = split(ref[start + k])
    widen(low, 2, pair, 0, 6)
    widen(high, 0, pair, 6, 4)

    def rows(g, _):
        back = own_terms(tab, g, PAIR + LATE)
        terms = far_terms(tab, g, PAIR, PAIR_AT, no_terms())
        lefts = lambda left: wide[g * SLOTS + left]
        for i, (left, number, index) in enumerate(back):
            back_buf[i] = halves(product(lefts(left), own[index]))
        for o in range(SLOTS):
            value = square_in[g * SLOTS + o]
            if o >= OWN and terms[o]:
                value = value + halves(chain(None, terms[o], lefts, pair, zeros))
            square[g * SLOTS + o] = value
        for i, (left, number, index) in enumerate(back):
            square[g * SLOTS + number] = square[g * SLOTS + number] + back_buf[i]
        for o in range(OWN):
            wsq[o] = split(square[g * SLOTS + o])
        for o in range(SLOTS):
            total = None
            for s in range(OWN):
                left = wsq[s]
                if o >= OWN:
                    left = masked(same_name(tab, g, s, o), left, zeros)
                total = add(total, product(left, wide[s * SLOTS + o]))
            cube[g * SLOTS + o] = halves(total)
        return 0

    lax.fori_loop(0, OWN, rows, 0)


def final_kernel(tab, wide, own_early, own_late, early, pair, square, cube, behind, ahead, beside, ham,
                 purified, virial, late, far_square, wsq, own_cube, back_buf, out_buf, sums, zeros, out_sem):
    zeros[...] = jnp.zeros_like(zeros)
    sums[...] = jnp.zeros_like(sums)
    for d, ref in ((3, behind), (4, ahead), (1, beside)):
        widen(ref, 0, late, LATE_AT[d], 10)

    def squares(g, _):
        terms = far_terms(tab, g, LATE, LATE_AT, no_terms())
        lefts = lambda left: wide[g * SLOTS + left]
        sums_of = [halves(chain(None, terms[o], lefts, late, zeros)) for o in range(OWN, SLOTS)]
        for i, total in enumerate(sums_of):
            value = square[g * SLOTS + OWN + i] + total
            far_square[g * 8 + i] = value
            wsq[g * 8 + i] = split(value)
        return 0

    lax.fori_loop(0, OWN, squares, 0, unroll=4)

    def rows(g, _):
        terms = far_terms(tab, g, PAIR, PAIR_AT, no_terms())
        early_terms = far_terms(tab, g, EARLY, EARLY_AT, no_terms())
        late_terms = far_terms(tab, g, LATE, LATE_AT, no_terms())
        lefts = lambda left: wsq[g * 8 + left - OWN]

        def finish(o, value):
            slot = tab[T_SLOT + g * SLOTS + o]
            out_buf[g, slot] = value
            for c in range(9):
                part = ham[c, g, slot].astype(jnp.float32) * value
                sums[c] += jnp.sum(part.reshape(EDGE // 8, 8, EDGE), axis=0)

        back = own_terms(tab, g, EARLY) + own_terms(tab, g, PAIR + LATE)
        backs = []
        for i, (left, number, index) in enumerate(back):
            own = own_early if i < len(EARLY) else own_late
            backs.append(halves(product(lefts(left), own[index])))
        cubes = []
        for o in range(OWN, SLOTS):
            if len(cubes) == 0:
                for i, total in enumerate(backs):
                    back_buf[i] = total
            total = chain(None, terms[o], lefts, pair, zeros)
            total = chain(total, early_terms[o], lefts, early, zeros)
            total = chain(total, late_terms[o], lefts, late, zeros)
            cubes.append(halves(total))
        for i, total in enumerate(cubes):
            o = OWN + i
            value = cube[g * SLOTS + o] + total
            finish(o, 3.0 * far_square[g * 8 + i] - 2.0 * value)
        for o in range(OWN):
            own_cube[o] = 3.0 * square[g * SLOTS + o] - 2.0 * cube[g * SLOTS + o]
        for i, (left, number, index) in enumerate(back):
            own_cube[number] = own_cube[number] - 2.0 * back_buf[i]
        for o in range(OWN):
            finish(o, own_cube[o])
        pltpu.make_async_copy(out_buf.at[g], purified.at[g], out_sem.at[g]).start()
        return 0

    lax.fori_loop(0, OWN, rows, 0, unroll=2)
    lane = lax.broadcasted_iota(jnp.int32, (8, EDGE), 1)
    line = jnp.zeros((8, EDGE), jnp.float32)
    for c in range(9):
        line = jnp.where(lane == c, jnp.sum(sums[c]), line)
    for i in range(N_DEV // 8):
        virial[pl.ds(i * 8, 8)] = line
    for g in range(OWN):
        pltpu.make_async_copy(out_buf.at[g], purified.at[g], out_sem.at[g]).wait()


def from_direction(d):
    dr, dc = DIRS[d]
    pairs = []
    for row in range(N_ROW):
        for col in range(N_COL):
            towards = 1 - 2 * (row & 1)
            there = (row + dr * towards) % N_ROW * N_COL + (col + dc) % N_COL
            pairs.append((there, row * N_COL + col))
    return pairs


ANY = pl.BlockSpec(memory_space=pl.ANY)
VMEM = pl.BlockSpec(memory_space=pltpu.VMEM)
SMEM = pl.BlockSpec(memory_space=pltpu.SMEM)
HBM = pl.BlockSpec(memory_space=pltpu.HBM)
F32 = jnp.float32
BF16 = jnp.bfloat16


def call(kernel, name, out, in_specs, out_specs, scratch, flops, moved, vmem=12):
    return pl.pallas_call(
        kernel,
        out_shape=out,
        in_specs=in_specs,
        out_specs=out_specs,
        scratch_shapes=scratch,
        compiler_params=pltpu.CompilerParams(vmem_limit_bytes=vmem << 20),
        cost_estimate=pl.CostEstimate(
            flops=flops * 2 * 4 * EDGE**3, bytes_accessed=moved << 20, transcendentals=0
        ),
        name=name,
    )


def blocks(*lead):
    return jax.ShapeDtypeStruct(lead + (EDGE, EDGE), F32)


def wides(*lead):
    return jax.ShapeDtypeStruct(lead + (EDGE, 2 * EDGE), BF16)


def wide_scratch(*lead):
    return pltpu.VMEM(lead + (EDGE, 2 * EDGE), BF16)


def scratch(*lead):
    return pltpu.VMEM(lead + (EDGE, EDGE), F32)


def body(density, pattern, ham_strain):
    dma = pltpu.SemaphoreType.DMA
    table = jax.ShapeDtypeStruct((T_SIZE,), jnp.int32)
    dens = density.reshape(OWN * SLOTS, EDGE, EDGE)
    tab, near_m, near_p, far_m, far_p, beside_own = call(
        first_kernel, "first", (table, blocks(10), blocks(10), blocks(8), blocks(8), blocks(2)),
        [HBM, HBM], (SMEM,) + (VMEM,) * 5,
        [scratch(OWN * SLOTS), pltpu.SMEM((SLOTS, N_DEV * OWN), jnp.int32), dma((2,))], 0, 10, 56,
    )(pattern.T, dens)
    near_ahead = lax.ppermute(near_m, AXES, from_direction(7))
    near_behind = lax.ppermute(near_p, AXES, from_direction(5))
    far_ahead = lax.ppermute(far_m, AXES, from_direction(2))
    far_behind = lax.ppermute(far_p, AXES, from_direction(0))
    beside_own = lax.ppermute(beside_own, AXES, from_direction(1))
    tab, wide, square = call(
        local_kernel, "local",
        (table, wides(OWN * SLOTS), blocks(OWN * SLOTS)),
        [SMEM, VMEM, SMEM, ANY], (SMEM,) + (VMEM,) * 2, [wide_scratch()], 400, 9,
    )(pattern.T, dens, tab, beside_own)
    late_m, late_p, beside = call(
        late_kernel, "late", (blocks(10), blocks(10), blocks(10)),
        [SMEM, VMEM, ANY], (VMEM,) * 3, [], 0, 3,
    )(tab, dens, square)
    pair_low, pair_high = call(
        second_kernel, "second", (blocks(8), blocks(8)),
        [SMEM] + [VMEM] * 3, (VMEM,) * 2, [], 0, 3,
    )(tab, dens, near_behind, near_ahead)
    late_ahead = lax.ppermute(late_m, AXES, from_direction(4))
    late_behind = lax.ppermute(late_p, AXES, from_direction(3))
    pair_low_in = lax.ppermute(pair_low, AXES, from_direction(6))
    pair_high_in = lax.ppermute(pair_high, AXES, from_direction(6))
    beside_in = lax.ppermute(beside, AXES, from_direction(1))
    own_early, early, square = call(
        early_kernel, "early",
        (wides(16), wides(N_EARLY), blocks(OWN * SLOTS)),
        [SMEM] + [VMEM] * 6 + [ANY] * 2, (VMEM,) * 3,
        [scratch(8), wide_scratch()], 0, 0,
    )(tab, wide, square, near_behind, near_ahead, far_behind, far_ahead, beside, late_m)
    own_late, pair, square, cube = call(
        pair_kernel, "pair",
        (wides(16), wides(N_PAIR), blocks(OWN * SLOTS), blocks(OWN * SLOTS)),
        [SMEM] + [VMEM] * 5, (VMEM,) * 4,
        [scratch(8), wide_scratch(OWN), wide_scratch()], 0, 0,
    )(tab, wide, square, pair_low_in, pair_high_in, beside_own)
    purified, line = call(
        final_kernel, "final",
        (blocks(OWN, SLOTS), jax.ShapeDtypeStruct((N_DEV, EDGE), F32)),
        [SMEM] + [VMEM] * 11, (ANY, VMEM),
        [
            wide_scratch(N_LATE), scratch(8 * OWN), wide_scratch(8 * OWN), scratch(OWN), scratch(8),
            scratch(OWN, SLOTS), pltpu.VMEM((9, 8, EDGE), F32), wide_scratch(), dma((OWN,)),
        ], 200, 30,
    )(tab, wide, own_early, own_late, early, pair, square, cube, late_behind, late_ahead, beside_in,
      ham_strain)
    total_blocks = N_DEV * OWN
    factor = 1.0 / math.sqrt(float(total_blocks * SLOTS * EDGE * EDGE))
    lines = lax.all_to_all(line, AXES, 0, 0, tiled=True)
    virial = (jnp.sum(lines, axis=0)[:9] * factor).reshape(3, 3)
    return purified, virial


def solution(mesh):
    in_specs = (P(AXES, None, None, None), P(), P(None, AXES, None, None, None))
    out_specs = (P(AXES, None, None, None), P())
    return jax.shard_map(body, mesh=mesh, in_specs=in_specs, out_specs=out_specs, check_vma=False)
```

```python
import math

import jax
import jax.numpy as jnp
from jax import lax
from jax.experimental import pallas as pl
from jax.experimental.pallas import tpu as pltpu
from jax.sharding import PartitionSpec as P

AXES = ("row", "col")
EDGE = 128
OWN = 4
SLOTS = 12
N_ROW = 16
N_COL = 8
N_DEV = N_ROW * N_COL

DIRS = ((-1, -1), (-1, 0), (-1, 1), (0, -1), (0, 1), (1, -1), (1, 0), (1, 1))


def near(a, b):
    return max(abs(a[0] - b[0]), abs(a[1] - b[1])) <= 1


COMMON = tuple(
    tuple(e for e in range(8) if e != d and near(DIRS[e], DIRS[d])) for d in range(8)
)
COUNT = tuple(2 + len(COMMON[d]) for d in range(8))
BACK = tuple(DIRS.index((dr, -dc)) for dr, dc in DIRS)
SEEN = tuple(
    tuple(
        DIRS.index(
            (
                (DIRS[e][0] - DIRS[d][0]) * (1 if DIRS[d][0] == 0 else -1),
                DIRS[e][1] - DIRS[d][1],
            )
        )
        for e in COMMON[d]
    )
    for d in range(8)
)

T_SLOT = 0
T_NAME = 48
T_LOW = 96
T_FAR = 104
T_SEND = 264
T_SIZE = 264 + 80
SEND_AT = tuple(T_SEND + 2 * sum(COUNT[:f]) for f in range(8))
CODES = tuple((dr + 1) * 3 + dc + 1 for dr, dc in DIRS)


def place(value, row, col):
    dev = value >> 2
    dr = ((dev >> 3) - row + 1) & (N_ROW - 1)
    dc = ((dev & (N_COL - 1)) - col + 1) & (N_COL - 1)
    return jnp.where(((row & 1) == 1) & (dr < 3), 2 - dr, dr), dc


def device_at(row, col, d):
    dr, dc = DIRS[d]
    towards = 1 - 2 * (row & 1)
    return ((row + dr * towards) & (N_ROW - 1)) * N_COL + ((col + dc) & (N_COL - 1))


def own_table(pat, row, col, tab):
    me = row * N_COL + col
    for l in range(OWN):
        for u in range(SLOTS):
            value = pat[u, me * OWN + l]
            dr, dc = place(value, row, col)
            code = dr * 3 + dc
            number = value & 3
            o = jnp.where(code == 4, number, code + jnp.where(code > 4, 3, 4))
            tab[T_SLOT + l * SLOTS + o] = u
            tab[T_NAME + l * SLOTS + o] = number


def named_rows(pat, other, me):
    named = []
    for j in range(OWN):
        number = jnp.int32(0)
        for u in range(SLOTS):
            value = pat[u, other * OWN + j]
            number = jnp.where((value >> 2) == me, value & 3, number)
        named.append(number)
    low = jnp.minimum(jnp.minimum(named[0], named[1]), jnp.minimum(named[2], named[3]))
    high = jnp.maximum(jnp.maximum(named[0], named[1]), jnp.maximum(named[2], named[3]))
    return low, high


def send_table(pat, row, col, tab):
    for f in range(8):
        d = BACK[f]
        rows = named_rows(pat, device_at(row, col, f), row * N_COL + col)
        for k, l in enumerate(rows):
            columns = [l, 4 + f] + [4 + e for e in SEEN[d]]
            for m, o in enumerate(columns):
                tab[SEND_AT[f] + k * COUNT[d] + m] = l * SLOTS + tab[T_SLOT + l * SLOTS + o]


def own_of(tab, f, k):
    return tab[SEND_AT[f] + k * COUNT[f] + 1]


def rest_of(tab, f, k):
    at = SEND_AT[f] + k * COUNT[f]
    return [tab[at]] + [tab[at + m] for m in range(2, COUNT[f])]


def fill(out, tab, dens, f, low=0, high=12):
    numbers = [own_of(tab, f, k) for k in range(2)] + rest_of(tab, f, 0) + rest_of(tab, f, 1)
    for i, n in enumerate(numbers[low:high]):
        out[i] = dens[n]


def first_kernel(pat_in, dens_in, tab, near_m, near_p, far_m, far_p, beside, dens, pat, sem):
    pat_load = pltpu.make_async_copy(pat_in, pat, sem.at[OWN])
    pat_load.start()
    loads = []
    for g in range(OWN):
        rows = pl.ds(g * SLOTS, SLOTS)
        loads.append(pltpu.make_async_copy(dens_in.at[rows], dens.at[rows], sem.at[g]))
        loads[g].start()
    pat_load.wait()
    row = lax.axis_index("row")
    col = lax.axis_index("col")
    own_table(pat, row, col, tab)
    send_table(pat, row, col, tab)
    for load in loads:
        load.wait()
    for out, f, edge in ((near_m, 5, 3), (near_p, 7, 4)):
        fill(out, tab, dens, f)
        for k in range(2):
            out[8 + k] = dens[own_of(tab, edge, k)]
    for out, f in ((far_m, 0), (far_p, 2)):
        fill(out, tab, dens, f)
    fill(beside, tab, dens, 1, 0, 2)


def late_kernel(tab, dens, *refs):
    for f, out in zip((3, 4, 1), refs[1:]):
        fill(out, tab, dens, f, 2, 12)


def second_kernel(tab, dens, behind, ahead, *refs):
    pair_low, pair_high = refs
    fill(pair_low, tab, dens, 6, 0, 8)
    fill(pair_high, tab, dens, 6, 8, 12)
    for k in range(2):
        pair_high[4 + k] = behind[8 + k]
        pair_high[6 + k] = ahead[8 + k]


def far_table(pat, row, col, tab):
    for d in range(8):
        names = [tab[T_NAME + l * SLOTS + 4 + d] for l in range(OWN)]
        low = jnp.minimum(jnp.minimum(names[0], names[1]), jnp.minimum(names[2], names[3]))
        high = jnp.maximum(jnp.maximum(names[0], names[1]), jnp.maximum(names[2], names[3]))
        tab[T_LOW + d] = low
        other = device_at(row, col, d)
        for k, l in enumerate((low, high)):
            for u in range(SLOTS):
                value = pat[u, other * OWN + l]
                dr, dc = place(value, row, col)
                code = jnp.where((dr < 3) & (dc < 3), dr * 3 + dc, 9)
                tab[T_FAR + (2 * d + k) * 10 + code] = value & 3


def split(value):
    high = value.astype(jnp.bfloat16)
    low = (value - high.astype(jnp.float32)).astype(jnp.bfloat16)
    return jnp.concatenate([high, low], axis=1)


def product(left, right):
    return jnp.dot(
        left, jnp.concatenate([right, right], axis=0), preferred_element_type=jnp.float32
    )


def halves(value):
    return value[:, :EDGE] + value[:, EDGE:]


def bit(tab, g, d):
    return jnp.where(tab[T_NAME + g * SLOTS + 4 + d] == tab[T_LOW + d], 0, 1)


def local_kernel(pat, dens, tab_in, after, tab, wide, square, zeros):
    del after
    row = lax.axis_index("row")
    col = lax.axis_index("col")
    for i in range(T_LOW):
        tab[i] = tab_in[i]
    for i in range(T_SEND, T_SIZE):
        tab[i] = tab_in[i]
    far_table(pat, row, col, tab)
    zeros[...] = jnp.zeros_like(zeros)

    def widen(i, _):
        wide[i] = split(dens[i // SLOTS * SLOTS + tab[T_SLOT + i]])
        return 0

    lax.fori_loop(0, OWN * SLOTS, widen, 0)

    def rows(g, _):
        for t in range(SLOTS):
            total = None
            for s in range(OWN):
                left = wide[g * SLOTS + s]
                if t >= OWN:
                    left = masked(same_name(tab, g, s, t), left, zeros)
                total = add(total, product(left, wide[s * SLOTS + t]))
            square[g * SLOTS + t] = halves(total)
        return 0

    lax.fori_loop(0, OWN, rows, 0)


def masked(match, left, zeros):
    if match is None:
        return left
    return jnp.where(match, left, zeros[...])


def same_name(tab, g, s, o):
    return bit(tab, g, o - OWN) == bit(tab, s, o - OWN)


def add(total, term):
    return term if total is None else total + term


def own_terms(tab, g, dirs):
    out = []
    for d in dirs:
        b = bit(tab, g, d)
        out.append((4 + d, tab[T_FAR + (2 * d + b) * 10 + 4], 2 * d + b))
    return out


def far_terms(tab, g, dirs, at, terms):
    for d in dirs:
        b = bit(tab, g, d)
        base = at[d] + b * (COUNT[d] - 1)
        info = T_FAR + (2 * d + b) * 10
        terms[4 + d].append((4 + d, None, base))
        for j, e in enumerate(COMMON[d]):
            match = tab[info + CODES[e]] == tab[T_NAME + g * SLOTS + 4 + e]
            terms[4 + e].append((4 + d, match, base + 1 + j))
    return terms


def no_terms():
    return {o: [] for o in range(OWN, SLOTS)}


def offsets(dirs):
    out, total = {}, 0
    for d in dirs:
        out[d] = total
        total += 2 * (COUNT[d] - 1)
    return out, total


EARLY = (0, 2, 5, 7)
PAIR = (6,)
BEHIND = (3,)
LATE = (4, 1)
EARLY_AT, N_EARLY = offsets(EARLY)
PAIR_AT, N_PAIR = offsets(PAIR)
LATE_AT, N_LATE = offsets(LATE)
BEHIND_AT, N_BEHIND = offsets(BEHIND)
READY = 5


def widen(ref, start, out, at, count):
    def one(i, _):
        out[at + i] = split(ref[start + i])
        return 0

    lax.fori_loop(0, count, one, 0, unroll=2)


def chain(total, listed, lefts, rights, zeros):
    for left, match, index in listed:
        total = add(total, product(masked(match, lefts(left), zeros), rights[index]))
    return total


def early_kernel(tab, wide, square_in, near_m, near_p, far_m, far_p, after, also,
                 own, early, square, back_buf, zeros):
    del after, also
    zeros[...] = jnp.zeros_like(zeros)
    for d, ref in ((0, far_m), (2, far_p), (5, near_m), (7, near_p)):
        for k in range(2):
            own[2 * d + k] = split(ref[k])
        widen(ref, 2, early, EARLY_AT[d], 2 * (COUNT[d] - 1))

    def rows(g, _):
        back = own_terms(tab, g, EARLY)
        terms = far_terms(tab, g, EARLY, EARLY_AT, no_terms())
        lefts = lambda left: wide[g * SLOTS + left]
        for i, (left, number, index) in enumerate(back):
            back_buf[i] = halves(product(lefts(left), own[index]))
        for o in range(SLOTS):
            value = square_in[g * SLOTS + o]
            if o >= OWN and terms[o]:
                value = value + halves(chain(None, terms[o], lefts, early, zeros))
            square[g * SLOTS + o] = value
        for i, (left, number, index) in enumerate(back):
            square[g * SLOTS + number] = square[g * SLOTS + number] + back_buf[i]
        return 0

    lax.fori_loop(0, OWN, rows, 0)


def pair_kernel(tab, wide, square_in, low, high, beside,
                own, pair, square, cube, back_buf, wsq, zeros):
    zeros[...] = jnp.zeros_like(zeros)
    for d, ref, start in ((6, low, 0), (1, beside, 0), (3, high, 4), (4, high, 6)):
        for k in range(2):
            own[2 * d + k] = split(ref[start + k])
    widen(low, 2, pair, 0, 6)
    widen(high, 0, pair, 6, 4)

    def rows(g, _):
        back = own_terms(tab, g, PAIR + BEHIND + LATE)
        terms = far_terms(tab, g, PAIR, PAIR_AT, no_terms())
        lefts = lambda left: wide[g * SLOTS + left]
        for i, (left, number, index) in enumerate(back):
            back_buf[i] = halves(product(lefts(left), own[index]))
        for o in range(SLOTS):
            value = square_in[g * SLOTS + o]
            if o >= OWN and terms[o]:
                value = value + halves(chain(None, terms[o], lefts, pair, zeros))
            square[g * SLOTS + o] = value
        for i, (left, number, index) in enumerate(back):
            square[g * SLOTS + number] = square[g * SLOTS + number] + back_buf[i]
        for o in range(OWN):
            wsq[o] = split(square[g * SLOTS + o])
        for o in range(SLOTS):
            total = None
            for s in range(OWN):
                left = wsq[s]
                if o >= OWN:
                    left = masked(same_name(tab, g, s, o), left, zeros)
                total = add(total, product(left, wide[s * SLOTS + o]))
            cube[g * SLOTS + o] = halves(total)
        return 0

    lax.fori_loop(0, OWN, rows, 0)


def behind_kernel(tab, wide, square_in, cube_in, own_early, early, ref, behind, square, cube, zeros):
    zeros[...] = jnp.zeros_like(zeros)
    widen(ref, 0, behind, 0, N_BEHIND)

    def rows(g, _):
        terms = far_terms(tab, g, BEHIND, BEHIND_AT, no_terms())
        lefts = lambda left: wide[g * SLOTS + left]
        for o in range(SLOTS):
            value = square_in[g * SLOTS + o]
            if o >= OWN and terms[o]:
                value = value + halves(chain(None, terms[o], lefts, behind, zeros))
            square[g * SLOTS + o] = value
        left = split(square[g * SLOTS + OWN + READY])
        ((_, number, index),) = own_terms(tab, g, (READY,))
        ready = far_terms(tab, g, (READY,), EARLY_AT, no_terms())
        for o in range(SLOTS):
            value = cube_in[g * SLOTS + o]
            if o >= OWN and ready[o]:
                value = value + halves(chain(None, ready[o], lambda _: left, early, zeros))
            cube[g * SLOTS + o] = value
        at = g * SLOTS + number
        cube[at] = cube[at] + halves(product(left, own_early[index]))
        return 0

    lax.fori_loop(0, OWN, rows, 0)


def final_kernel(tab, wide, own_early, own_late, early, pair, behind, square, cube, ahead, beside, ham,
                 purified, virial, late, far_square, wsq, own_cube, back_buf, out_buf, sums, zeros, out_sem):
    zeros[...] = jnp.zeros_like(zeros)
    sums[...] = jnp.zeros_like(sums)
    for d, ref in ((4, ahead), (1, beside)):
        widen(ref, 0, late, LATE_AT[d], 10)

    def squares(g, _):
        terms = far_terms(tab, g, LATE, LATE_AT, no_terms())
        lefts = lambda left: wide[g * SLOTS + left]
        sums_of = [
            halves(chain(None, terms[o], lefts, late, zeros)) if terms[o] else 0.0
            for o in range(OWN, SLOTS)
        ]
        for i, total in enumerate(sums_of):
            value = square[g * SLOTS + OWN + i] + total
            far_square[g * 8 + i] = value
            wsq[g * 8 + i] = split(value)
        return 0

    lax.fori_loop(0, OWN, squares, 0, unroll=4)

    def rows(g, _):
        terms = far_terms(tab, g, PAIR, PAIR_AT, no_terms())
        rest = tuple(d for d in EARLY if d != READY)
        early_terms = far_terms(tab, g, rest, EARLY_AT, no_terms())
        behind_terms = far_terms(tab, g, BEHIND, BEHIND_AT, no_terms())
        late_terms = far_terms(tab, g, LATE, LATE_AT, no_terms())
        lefts = lambda left: wsq[g * 8 + left - OWN]

        def finish(o, value):
            slot = tab[T_SLOT + g * SLOTS + o]
            out_buf[g, slot] = value
            for c in range(9):
                part = ham[c, g, slot].astype(jnp.float32) * value
                sums[c] += jnp.sum(part.reshape(EDGE // 8, 8, EDGE), axis=0)

        back = own_terms(tab, g, rest) + own_terms(tab, g, PAIR + BEHIND + LATE)
        backs = []
        for i, (left, number, index) in enumerate(back):
            own = own_early if i < len(rest) else own_late
            backs.append(halves(product(lefts(left), own[index])))
        cubes = []
        for o in range(OWN, SLOTS):
            if len(cubes) == 0:
                for i, total in enumerate(backs):
                    back_buf[i] = total
            total = chain(None, terms[o], lefts, pair, zeros)
            total = chain(total, early_terms[o], lefts, early, zeros)
            total = chain(total, behind_terms[o], lefts, behind, zeros)
            total = chain(total, late_terms[o], lefts, late, zeros)
            cubes.append(halves(total))
        for i, total in enumerate(cubes):
            o = OWN + i
            value = cube[g * SLOTS + o] + total
            finish(o, 3.0 * far_square[g * 8 + i] - 2.0 * value)
        for o in range(OWN):
            own_cube[o] = 3.0 * square[g * SLOTS + o] - 2.0 * cube[g * SLOTS + o]
        for i, (left, number, index) in enumerate(back):
            own_cube[number] = own_cube[number] - 2.0 * back_buf[i]
        for o in range(OWN):
            finish(o, own_cube[o])
        pltpu.make_async_copy(out_buf.at[g], purified.at[g], out_sem.at[g]).start()
        return 0

    lax.fori_loop(0, OWN, rows, 0, unroll=2)
    lane = lax.broadcasted_iota(jnp.int32, (8, EDGE), 1)
    line = jnp.zeros((8, EDGE), jnp.float32)
    for c in range(9):
        line = jnp.where(lane == c, jnp.sum(sums[c]), line)
    for i in range(N_DEV // 8):
        virial[pl.ds(i * 8, 8)] = line
    for g in range(OWN):
        pltpu.make_async_copy(out_buf.at[g], purified.at[g], out_sem.at[g]).wait()


def from_direction(d):
    dr, dc = DIRS[d]
    pairs = []
    for row in range(N_ROW):
        for col in range(N_COL):
            towards = 1 - 2 * (row & 1)
            there = (row + dr * towards) % N_ROW * N_COL + (col + dc) % N_COL
            pairs.append((there, row * N_COL + col))
    return pairs


ANY = pl.BlockSpec(memory_space=pl.ANY)
VMEM = pl.BlockSpec(memory_space=pltpu.VMEM)
SMEM = pl.BlockSpec(memory_space=pltpu.SMEM)
HBM = pl.BlockSpec(memory_space=pltpu.HBM)
F32 = jnp.float32
BF16 = jnp.bfloat16


def call(kernel, name, out, in_specs, out_specs, scratch, flops, moved, vmem=12):
    return pl.pallas_call(
        kernel,
        out_shape=out,
        in_specs=in_specs,
        out_specs=out_specs,
        scratch_shapes=scratch,
        compiler_params=pltpu.CompilerParams(vmem_limit_bytes=vmem << 20),
        cost_estimate=pl.CostEstimate(
            flops=flops * 2 * 4 * EDGE**3, bytes_accessed=moved << 20, transcendentals=0
        ),
        name=name,
    )


def blocks(*lead):
    return jax.ShapeDtypeStruct(lead + (EDGE, EDGE), F32)


def wides(*lead):
    return jax.ShapeDtypeStruct(lead + (EDGE, 2 * EDGE), BF16)


def wide_scratch(*lead):
    return pltpu.VMEM(lead + (EDGE, 2 * EDGE), BF16)


def scratch(*lead):
    return pltpu.VMEM(lead + (EDGE, EDGE), F32)


def body(density, pattern, ham_strain):
    dma = pltpu.SemaphoreType.DMA
    table = jax.ShapeDtypeStruct((T_SIZE,), jnp.int32)
    dens = density.reshape(OWN * SLOTS, EDGE, EDGE)
    tab, near_m, near_p, far_m, far_p, beside_own = call(
        first_kernel, "first", (table, blocks(10), blocks(10), blocks(8), blocks(8), blocks(2)),
        [HBM, HBM], (SMEM,) + (VMEM,) * 5,
        [scratch(OWN * SLOTS), pltpu.SMEM((SLOTS, N_DEV * OWN), jnp.int32), dma((OWN + 1,))], 0, 10, 56,
    )(pattern.T, dens)
    near_ahead = lax.ppermute(near_m, AXES, from_direction(7))
    near_behind = lax.ppermute(near_p, AXES, from_direction(5))
    far_ahead = lax.ppermute(far_m, AXES, from_direction(2))
    far_behind = lax.ppermute(far_p, AXES, from_direction(0))
    beside_own = lax.ppermute(beside_own, AXES, from_direction(1))
    tab, wide, square = call(
        local_kernel, "local",
        (table, wides(OWN * SLOTS), blocks(OWN * SLOTS)),
        [SMEM, VMEM, SMEM, ANY], (SMEM,) + (VMEM,) * 2, [wide_scratch()], 400, 9,
    )(pattern.T, dens, tab, beside_own)
    late_m, late_p, beside = call(
        late_kernel, "late", (blocks(10), blocks(10), blocks(10)),
        [SMEM, VMEM, ANY], (VMEM,) * 3, [], 0, 3,
    )(tab, dens, square)
    pair_low, pair_high = call(
        second_kernel, "second", (blocks(8), blocks(8)),
        [SMEM] + [VMEM] * 3, (VMEM,) * 2, [], 0, 3,
    )(tab, dens, near_behind, near_ahead)
    late_ahead = lax.ppermute(late_m, AXES, from_direction(4))
    late_behind = lax.ppermute(late_p, AXES, from_direction(3))
    pair_low_in = lax.ppermute(pair_low, AXES, from_direction(6))
    pair_high_in = lax.ppermute(pair_high, AXES, from_direction(6))
    beside_in = lax.ppermute(beside, AXES, from_direction(1))
    own_early, early, square = call(
        early_kernel, "early",
        (wides(16), wides(N_EARLY), blocks(OWN * SLOTS)),
        [SMEM] + [VMEM] * 6 + [ANY] * 2, (VMEM,) * 3,
        [scratch(8), wide_scratch()], 0, 0,
    )(tab, wide, square, near_behind, near_ahead, far_behind, far_ahead, beside, late_m)
    own_late, pair, square, cube = call(
        pair_kernel, "pair",
        (wides(16), wides(N_PAIR), blocks(OWN * SLOTS), blocks(OWN * SLOTS)),
        [SMEM] + [VMEM] * 5, (VMEM,) * 4,
        [scratch(8), wide_scratch(OWN), wide_scratch()], 0, 0,
    )(tab, wide, square, pair_low_in, pair_high_in, beside_own)
    behind, square, cube = call(
        behind_kernel, "behind",
        (wides(N_BEHIND), blocks(OWN * SLOTS), blocks(OWN * SLOTS)),
        [SMEM] + [VMEM] * 6, (VMEM,) * 3, [wide_scratch()], 0, 0,
    )(tab, wide, square, cube, own_early, early, late_behind)
    purified, line = call(
        final_kernel, "final",
        (blocks(OWN, SLOTS), jax.ShapeDtypeStruct((N_DEV, EDGE), F32)),
        [SMEM] + [VMEM] * 11, (ANY, VMEM),
        [
            wide_scratch(N_LATE), scratch(8 * OWN), wide_scratch(8 * OWN), scratch(OWN), scratch(8),
            scratch(OWN, SLOTS), pltpu.VMEM((9, 8, EDGE), F32), wide_scratch(), dma((OWN,)),
        ], 200, 30,
    )(tab, wide, own_early, own_late, early, pair, behind, square, cube, late_ahead, beside_in,
      ham_strain)
    total_blocks = N_DEV * OWN
    factor = 1.0 / math.sqrt(float(total_blocks * SLOTS * EDGE * EDGE))
    lines = lax.all_to_all(line, AXES, 0, 0, tiled=True)
    virial = (jnp.sum(lines, axis=0)[:9] * factor).reshape(3, 3)
    return purified, virial


def solution(mesh):
    in_specs = (P(AXES, None, None, None), P(), P(None, AXES, None, None, None))
    out_specs = (P(AXES, None, None, None), P())
    return jax.shard_map(body, mesh=mesh, in_specs=in_specs, out_specs=out_specs, check_vma=False)
```

```python
import functools
import math

import jax
import jax.numpy as jnp
from jax import lax
from jax.experimental import pallas as pl
from jax.experimental.pallas import tpu as pltpu
from jax.sharding import PartitionSpec as P

AXES = ("row", "col")
EDGE = 128
OWN = 4
SLOTS = 12
N_ROW = 16
N_COL = 8
N_DEV = N_ROW * N_COL

DIRS = ((-1, -1), (-1, 0), (-1, 1), (0, -1), (0, 1), (1, -1), (1, 0), (1, 1))


def near(a, b):
    return max(abs(a[0] - b[0]), abs(a[1] - b[1])) <= 1


COMMON = tuple(
    tuple(e for e in range(8) if e != d and near(DIRS[e], DIRS[d])) for d in range(8)
)
COUNT = tuple(2 + len(COMMON[d]) for d in range(8))
BACK = tuple(DIRS.index((dr, -dc)) for dr, dc in DIRS)
SEEN = tuple(
    tuple(
        DIRS.index(
            (
                (DIRS[e][0] - DIRS[d][0]) * (1 if DIRS[d][0] == 0 else -1),
                DIRS[e][1] - DIRS[d][1],
            )
        )
        for e in COMMON[d]
    )
    for d in range(8)
)

T_SLOT = 0
T_NAME = 48
T_LOW = 96
T_FAR = 104
T_SEND = 264
T_SIZE = 264 + 80
SEND_AT = tuple(T_SEND + 2 * sum(COUNT[:f]) for f in range(8))
CODES = tuple((dr + 1) * 3 + dc + 1 for dr, dc in DIRS)


def place(value, row, col):
    dev = value >> 2
    dr = ((dev >> 3) - row + 1) & (N_ROW - 1)
    dc = ((dev & (N_COL - 1)) - col + 1) & (N_COL - 1)
    return jnp.where(((row & 1) == 1) & (dr < 3), 2 - dr, dr), dc


def device_at(row, col, d):
    dr, dc = DIRS[d]
    towards = 1 - 2 * (row & 1)
    return ((row + dr * towards) & (N_ROW - 1)) * N_COL + ((col + dc) & (N_COL - 1))


def own_table(pat, row, col, tab):
    me = row * N_COL + col
    for l in range(OWN):
        for u in range(SLOTS):
            value = pat[u, me * OWN + l]
            dr, dc = place(value, row, col)
            code = dr * 3 + dc
            number = value & 3
            o = jnp.where(code == 4, number, code + jnp.where(code > 4, 3, 4))
            tab[T_SLOT + l * SLOTS + o] = u
            tab[T_NAME + l * SLOTS + o] = number


def named_rows(pat, other, me):
    named = []
    for j in range(OWN):
        number = jnp.int32(0)
        for u in range(SLOTS):
            value = pat[u, other * OWN + j]
            number = jnp.where((value >> 2) == me, value & 3, number)
        named.append(number)
    low = jnp.minimum(jnp.minimum(named[0], named[1]), jnp.minimum(named[2], named[3]))
    high = jnp.maximum(jnp.maximum(named[0], named[1]), jnp.maximum(named[2], named[3]))
    return low, high


def send_table(pat, row, col, tab):
    for f in range(8):
        d = BACK[f]
        rows = named_rows(pat, device_at(row, col, f), row * N_COL + col)
        for k, l in enumerate(rows):
            columns = [l, 4 + f] + [4 + e for e in SEEN[d]]
            for m, o in enumerate(columns):
                tab[SEND_AT[f] + k * COUNT[d] + m] = l * SLOTS + tab[T_SLOT + l * SLOTS + o]


def own_of(tab, f, k):
    return tab[SEND_AT[f] + k * COUNT[f] + 1]


def rest_of(tab, f, k):
    at = SEND_AT[f] + k * COUNT[f]
    return [tab[at]] + [tab[at + m] for m in range(2, COUNT[f])]


def fill(out, tab, dens, f, low=0, high=12):
    numbers = [own_of(tab, f, k) for k in range(2)] + rest_of(tab, f, 0) + rest_of(tab, f, 1)
    for i, n in enumerate(numbers[low:high]):
        out[i] = dens[n]


def first_kernel(pat_in, dens_in, tab, near_m, near_p, far_m, far_p, beside, dens, pat, sem):
    pat_load = pltpu.make_async_copy(pat_in, pat, sem.at[OWN])
    pat_load.start()
    loads = []
    for g in range(OWN):
        rows = pl.ds(g * SLOTS, SLOTS)
        loads.append(pltpu.make_async_copy(dens_in.at[rows], dens.at[rows], sem.at[g]))
        loads[g].start()
    pat_load.wait()
    row = lax.axis_index("row")
    col = lax.axis_index("col")
    own_table(pat, row, col, tab)
    send_table(pat, row, col, tab)
    for load in loads:
        load.wait()
    for out, f, edge in ((near_m, 5, 3), (near_p, 7, 4)):
        fill(out, tab, dens, f)
        for k in range(2):
            out[8 + k] = dens[own_of(tab, edge, k)]
    for out, f in ((far_m, 0), (far_p, 2)):
        fill(out, tab, dens, f)
    fill(beside, tab, dens, 1, 0, 2)


def late_kernel(dirs, tab, dens, *refs):
    for f, out in zip(dirs, refs[1:]):
        fill(out, tab, dens, f, 2, 12)


def second_kernel(tab, dens, behind, ahead, *refs):
    pair_low, pair_high = refs
    fill(pair_low, tab, dens, 6, 0, 8)
    fill(pair_high, tab, dens, 6, 8, 12)
    for k in range(2):
        pair_high[4 + k] = behind[8 + k]
        pair_high[6 + k] = ahead[8 + k]


def far_table(pat, row, col, tab):
    for d in range(8):
        names = [tab[T_NAME + l * SLOTS + 4 + d] for l in range(OWN)]
        low = jnp.minimum(jnp.minimum(names[0], names[1]), jnp.minimum(names[2], names[3]))
        high = jnp.maximum(jnp.maximum(names[0], names[1]), jnp.maximum(names[2], names[3]))
        tab[T_LOW + d] = low
        other = device_at(row, col, d)
        for k, l in enumerate((low, high)):
            for u in range(SLOTS):
                value = pat[u, other * OWN + l]
                dr, dc = place(value, row, col)
                code = jnp.where((dr < 3) & (dc < 3), dr * 3 + dc, 9)
                tab[T_FAR + (2 * d + k) * 10 + code] = value & 3


def split(value):
    high = value.astype(jnp.bfloat16)
    low = (value - high.astype(jnp.float32)).astype(jnp.bfloat16)
    return jnp.concatenate([high, low], axis=1)


def product(left, right):
    return jnp.dot(
        left, jnp.concatenate([right, right], axis=0), preferred_element_type=jnp.float32
    )


def halves(value):
    return value[:, :EDGE] + value[:, EDGE:]


def bit(tab, g, d):
    return jnp.where(tab[T_NAME + g * SLOTS + 4 + d] == tab[T_LOW + d], 0, 1)


def local_kernel(pat, dens, tab_in, after, tab, wide, square, zeros):
    del after
    row = lax.axis_index("row")
    col = lax.axis_index("col")
    for i in range(T_LOW):
        tab[i] = tab_in[i]
    for i in range(T_SEND, T_SIZE):
        tab[i] = tab_in[i]
    far_table(pat, row, col, tab)
    zeros[...] = jnp.zeros_like(zeros)

    def widen(i, _):
        wide[i] = split(dens[i // SLOTS * SLOTS + tab[T_SLOT + i]])
        return 0

    lax.fori_loop(0, OWN * SLOTS, widen, 0)

    def rows(g, _):
        for t in range(SLOTS):
            total = None
            for s in range(OWN):
                left = wide[g * SLOTS + s]
                if t >= OWN:
                    left = masked(same_name(tab, g, s, t), left, zeros)
                total = add(total, product(left, wide[s * SLOTS + t]))
            square[g * SLOTS + t] = halves(total)
        return 0

    lax.fori_loop(0, OWN, rows, 0)


def masked(match, left, zeros):
    if match is None:
        return left
    return jnp.where(match, left, zeros[...])


def same_name(tab, g, s, o):
    return bit(tab, g, o - OWN) == bit(tab, s, o - OWN)


def add(total, term):
    return term if total is None else total + term


def own_terms(tab, g, dirs):
    out = []
    for d in dirs:
        b = bit(tab, g, d)
        out.append((4 + d, tab[T_FAR + (2 * d + b) * 10 + 4], 2 * d + b))
    return out


def far_terms(tab, g, dirs, at, terms):
    for d in dirs:
        b = bit(tab, g, d)
        base = at[d] + b * (COUNT[d] - 1)
        info = T_FAR + (2 * d + b) * 10
        terms[4 + d].append((4 + d, None, base))
        for j, e in enumerate(COMMON[d]):
            match = tab[info + CODES[e]] == tab[T_NAME + g * SLOTS + 4 + e]
            terms[4 + e].append((4 + d, match, base + 1 + j))
    return terms


def no_terms():
    return {o: [] for o in range(OWN, SLOTS)}


def offsets(dirs):
    out, total = {}, 0
    for d in dirs:
        out[d] = total
        total += 2 * (COUNT[d] - 1)
    return out, total


EARLY = (0, 2, 5, 7)
PAIR = (6,)
BEHIND = (3,)
LATE = (4, 1)
EARLY_AT, N_EARLY = offsets(EARLY)
PAIR_AT, N_PAIR = offsets(PAIR)
LATE_AT, N_LATE = offsets(LATE)
BEHIND_AT, N_BEHIND = offsets(BEHIND)
READY = 5


def widen(ref, start, out, at, count):
    def one(i, _):
        out[at + i] = split(ref[start + i])
        return 0

    lax.fori_loop(0, count, one, 0, unroll=2)


def chain(total, listed, lefts, rights, zeros):
    for left, match, index in listed:
        total = add(total, product(masked(match, lefts(left), zeros), rights[index]))
    return total


def early_kernel(tab, wide, square_in, near_m, near_p, far_m, far_p, after, also,
                 own, early, square, back_buf, zeros):
    del after, also
    zeros[...] = jnp.zeros_like(zeros)
    for d, ref in ((0, far_m), (2, far_p), (5, near_m), (7, near_p)):
        for k in range(2):
            own[2 * d + k] = split(ref[k])
        widen(ref, 2, early, EARLY_AT[d], 2 * (COUNT[d] - 1))

    def rows(g, _):
        back = own_terms(tab, g, EARLY)
        terms = far_terms(tab, g, EARLY, EARLY_AT, no_terms())
        lefts = lambda left: wide[g * SLOTS + left]
        for i, (left, number, index) in enumerate(back):
            back_buf[i] = halves(product(lefts(left), own[index]))
        for o in range(SLOTS):
            value = square_in[g * SLOTS + o]
            if o >= OWN and terms[o]:
                value = value + halves(chain(None, terms[o], lefts, early, zeros))
            square[g * SLOTS + o] = value
        for i, (left, number, index) in enumerate(back):
            square[g * SLOTS + number] = square[g * SLOTS + number] + back_buf[i]
        return 0

    lax.fori_loop(0, OWN, rows, 0)


def pair_kernel(tab, wide, square_in, low, high, beside,
                own, pair, square, cube, back_buf, wsq, zeros):
    zeros[...] = jnp.zeros_like(zeros)
    for d, ref, start in ((6, low, 0), (1, beside, 0), (3, high, 4), (4, high, 6)):
        for k in range(2):
            own[2 * d + k] = split(ref[start + k])
    widen(low, 2, pair, 0, 6)
    widen(high, 0, pair, 6, 4)

    def rows(g, _):
        back = own_terms(tab, g, PAIR + BEHIND + LATE)
        terms = far_terms(tab, g, PAIR, PAIR_AT, no_terms())
        lefts = lambda left: wide[g * SLOTS + left]
        for i, (left, number, index) in enumerate(back):
            back_buf[i] = halves(product(lefts(left), own[index]))
        for o in range(SLOTS):
            value = square_in[g * SLOTS + o]
            if o >= OWN and terms[o]:
                value = value + halves(chain(None, terms[o], lefts, pair, zeros))
            square[g * SLOTS + o] = value
        for i, (left, number, index) in enumerate(back):
            square[g * SLOTS + number] = square[g * SLOTS + number] + back_buf[i]
        for o in range(OWN):
            wsq[o] = split(square[g * SLOTS + o])
        for o in range(SLOTS):
            total = None
            for s in range(OWN):
                left = wsq[s]
                if o >= OWN:
                    left = masked(same_name(tab, g, s, o), left, zeros)
                total = add(total, product(left, wide[s * SLOTS + o]))
            cube[g * SLOTS + o] = halves(total)
        return 0

    lax.fori_loop(0, OWN, rows, 0)


def behind_kernel(tab, wide, square_in, cube_in, own_early, early, ref, behind, square, cube, zeros):
    zeros[...] = jnp.zeros_like(zeros)
    widen(ref, 0, behind, 0, N_BEHIND)

    def rows(g, _):
        terms = far_terms(tab, g, BEHIND, BEHIND_AT, no_terms())
        lefts = lambda left: wide[g * SLOTS + left]
        for o in range(SLOTS):
            value = square_in[g * SLOTS + o]
            if o >= OWN and terms[o]:
                value = value + halves(chain(None, terms[o], lefts, behind, zeros))
            square[g * SLOTS + o] = value
        left = split(square[g * SLOTS + OWN + READY])
        ((_, number, index),) = own_terms(tab, g, (READY,))
        ready = far_terms(tab, g, (READY,), EARLY_AT, no_terms())
        for o in range(SLOTS):
            value = cube_in[g * SLOTS + o]
            if o >= OWN and ready[o]:
                value = value + halves(chain(None, ready[o], lambda _: left, early, zeros))
            cube[g * SLOTS + o] = value
        at = g * SLOTS + number
        cube[at] = cube[at] + halves(product(left, own_early[index]))
        return 0

    lax.fori_loop(0, OWN, rows, 0)


def final_kernel(tab, wide, own_early, own_late, early, pair, behind, square, cube, ahead, beside, ham,
                 purified, virial, late, far_square, wsq, own_cube, back_buf, out_buf, sums, zeros, out_sem):
    zeros[...] = jnp.zeros_like(zeros)
    sums[...] = jnp.zeros_like(sums)
    for d, ref in ((4, ahead), (1, beside)):
        widen(ref, 0, late, LATE_AT[d], 10)

    def squares(g, _):
        terms = far_terms(tab, g, LATE, LATE_AT, no_terms())
        lefts = lambda left: wide[g * SLOTS + left]
        sums_of = [
            halves(chain(None, terms[o], lefts, late, zeros)) if terms[o] else 0.0
            for o in range(OWN, SLOTS)
        ]
        for i, total in enumerate(sums_of):
            value = square[g * SLOTS + OWN + i] + total
            far_square[g * 8 + i] = value
            wsq[g * 8 + i] = split(value)
        return 0

    lax.fori_loop(0, OWN, squares, 0, unroll=4)

    def rows(g, _):
        terms = far_terms(tab, g, PAIR, PAIR_AT, no_terms())
        rest = tuple(d for d in EARLY if d != READY)
        early_terms = far_terms(tab, g, rest, EARLY_AT, no_terms())
        behind_terms = far_terms(tab, g, BEHIND, BEHIND_AT, no_terms())
        late_terms = far_terms(tab, g, LATE, LATE_AT, no_terms())
        lefts = lambda left: wsq[g * 8 + left - OWN]

        def finish(o, value):
            slot = tab[T_SLOT + g * SLOTS + o]
            out_buf[g, slot] = value
            block = pltpu.make_async_copy(
                out_buf.at[g, slot], purified.at[g, slot], out_sem.at[g]
            )
            block.start()
            for c in range(9):
                part = ham[c, g, slot].astype(jnp.float32) * value
                sums[c] += jnp.sum(part.reshape(EDGE // 8, 8, EDGE), axis=0)

        back = own_terms(tab, g, rest) + own_terms(tab, g, PAIR + BEHIND + LATE)
        backs = []
        for i, (left, number, index) in enumerate(back):
            own = own_early if i < len(rest) else own_late
            backs.append(halves(product(lefts(left), own[index])))
        cubes = []
        for o in range(OWN, SLOTS):
            if len(cubes) == 0:
                for i, total in enumerate(backs):
                    back_buf[i] = total
            total = chain(None, terms[o], lefts, pair, zeros)
            total = chain(total, early_terms[o], lefts, early, zeros)
            total = chain(total, behind_terms[o], lefts, behind, zeros)
            total = chain(total, late_terms[o], lefts, late, zeros)
            cubes.append(halves(total))
        for i, total in enumerate(cubes):
            o = OWN + i
            value = cube[g * SLOTS + o] + total
            finish(o, 3.0 * far_square[g * 8 + i] - 2.0 * value)
        for o in range(OWN):
            own_cube[o] = 3.0 * square[g * SLOTS + o] - 2.0 * cube[g * SLOTS + o]
        for i, (left, number, index) in enumerate(back):
            own_cube[number] = own_cube[number] - 2.0 * back_buf[i]
        for o in range(OWN):
            finish(o, own_cube[o])
        return 0

    lax.fori_loop(0, OWN, rows, 0, unroll=2)
    lane = lax.broadcasted_iota(jnp.int32, (8, EDGE), 1)
    line = jnp.zeros((8, EDGE), jnp.float32)
    for c in range(9):
        line = jnp.where(lane == c, jnp.sum(sums[c]), line)
    for i in range(N_DEV // 8):
        virial[pl.ds(i * 8, 8)] = line
    for g in range(OWN):
        pltpu.make_async_copy(out_buf.at[g], purified.at[g], out_sem.at[g]).wait()


def from_direction(d):
    dr, dc = DIRS[d]
    pairs = []
    for row in range(N_ROW):
        for col in range(N_COL):
            towards = 1 - 2 * (row & 1)
            there = (row + dr * towards) % N_ROW * N_COL + (col + dc) % N_COL
            pairs.append((there, row * N_COL + col))
    return pairs


ANY = pl.BlockSpec(memory_space=pl.ANY)
VMEM = pl.BlockSpec(memory_space=pltpu.VMEM)
SMEM = pl.BlockSpec(memory_space=pltpu.SMEM)
HBM = pl.BlockSpec(memory_space=pltpu.HBM)
F32 = jnp.float32
BF16 = jnp.bfloat16


def call(kernel, name, out, in_specs, out_specs, scratch, flops, moved, vmem=12):
    return pl.pallas_call(
        kernel,
        out_shape=out,
        in_specs=in_specs,
        out_specs=out_specs,
        scratch_shapes=scratch,
        compiler_params=pltpu.CompilerParams(vmem_limit_bytes=vmem << 20),
        cost_estimate=pl.CostEstimate(
            flops=flops * 2 * 4 * EDGE**3, bytes_accessed=moved << 20, transcendentals=0
        ),
        name=name,
    )


def blocks(*lead):
    return jax.ShapeDtypeStruct(lead + (EDGE, EDGE), F32)


def wides(*lead):
    return jax.ShapeDtypeStruct(lead + (EDGE, 2 * EDGE), BF16)


def wide_scratch(*lead):
    return pltpu.VMEM(lead + (EDGE, 2 * EDGE), BF16)


def scratch(*lead):
    return pltpu.VMEM(lead + (EDGE, EDGE), F32)


def body(density, pattern, ham_strain):
    dma = pltpu.SemaphoreType.DMA
    table = jax.ShapeDtypeStruct((T_SIZE,), jnp.int32)
    dens = density.reshape(OWN * SLOTS, EDGE, EDGE)
    tab, near_m, near_p, far_m, far_p, beside_own = call(
        first_kernel, "first", (table, blocks(10), blocks(10), blocks(8), blocks(8), blocks(2)),
        [HBM, HBM], (SMEM,) + (VMEM,) * 5,
        [scratch(OWN * SLOTS), pltpu.SMEM((SLOTS, N_DEV * OWN), jnp.int32), dma((OWN + 1,))], 0, 10, 56,
    )(pattern.T, dens)
    near_ahead = lax.ppermute(near_m, AXES, from_direction(7))
    near_behind = lax.ppermute(near_p, AXES, from_direction(5))
    far_ahead = lax.ppermute(far_m, AXES, from_direction(2))
    far_behind = lax.ppermute(far_p, AXES, from_direction(0))
    beside_own = lax.ppermute(beside_own, AXES, from_direction(1))
    late_p = call(
        functools.partial(late_kernel, (4,)), "late", blocks(10),
        [SMEM, VMEM, ANY], VMEM, [], 0, 1,
    )(tab, dens, beside_own)
    tab, wide, square = call(
        local_kernel, "local",
        (table, wides(OWN * SLOTS), blocks(OWN * SLOTS)),
        [SMEM, VMEM, SMEM, ANY], (SMEM,) + (VMEM,) * 2, [wide_scratch()], 400, 9,
    )(pattern.T, dens, tab, late_p)
    late_m, beside = call(
        functools.partial(late_kernel, (3, 1)), "later", (blocks(10), blocks(10)),
        [SMEM, VMEM, ANY], (VMEM,) * 2, [], 0, 2,
    )(tab, dens, square)
    pair_low, pair_high = call(
        second_kernel, "second", (blocks(8), blocks(8)),
        [SMEM] + [VMEM] * 3, (VMEM,) * 2, [], 0, 3,
    )(tab, dens, near_behind, near_ahead)
    late_ahead = lax.ppermute(late_m, AXES, from_direction(4))
    late_behind = lax.ppermute(late_p, AXES, from_direction(3))
    pair_low_in = lax.ppermute(pair_low, AXES, from_direction(6))
    pair_high_in = lax.ppermute(pair_high, AXES, from_direction(6))
    beside_in = lax.ppermute(beside, AXES, from_direction(1))
    own_early, early, square = call(
        early_kernel, "early",
        (wides(16), wides(N_EARLY), blocks(OWN * SLOTS)),
        [SMEM] + [VMEM] * 6 + [ANY] * 2, (VMEM,) * 3,
        [scratch(8), wide_scratch()], 0, 0,
    )(tab, wide, square, near_behind, near_ahead, far_behind, far_ahead, beside, late_m)
    own_late, pair, square, cube = call(
        pair_kernel, "pair",
        (wides(16), wides(N_PAIR), blocks(OWN * SLOTS), blocks(OWN * SLOTS)),
        [SMEM] + [VMEM] * 5, (VMEM,) * 4,
        [scratch(8), wide_scratch(OWN), wide_scratch()], 0, 0,
    )(tab, wide, square, pair_low_in, pair_high_in, beside_own)
    behind, square, cube = call(
        behind_kernel, "behind",
        (wides(N_BEHIND), blocks(OWN * SLOTS), blocks(OWN * SLOTS)),
        [SMEM] + [VMEM] * 6, (VMEM,) * 3, [wide_scratch()], 0, 0,
    )(tab, wide, square, cube, own_early, early, late_behind)
    purified, line = call(
        final_kernel, "final",
        (blocks(OWN, SLOTS), jax.ShapeDtypeStruct((N_DEV, EDGE), F32)),
        [SMEM] + [VMEM] * 11, (ANY, VMEM),
        [
            wide_scratch(N_LATE), scratch(8 * OWN), wide_scratch(8 * OWN), scratch(OWN), scratch(8),
            scratch(OWN, SLOTS), pltpu.VMEM((9, 8, EDGE), F32), wide_scratch(), dma((OWN,)),
        ], 200, 30,
    )(tab, wide, own_early, own_late, early, pair, behind, square, cube, late_ahead, beside_in,
      ham_strain)
    total_blocks = N_DEV * OWN
    factor = 1.0 / math.sqrt(float(total_blocks * SLOTS * EDGE * EDGE))
    lines = lax.all_to_all(line, AXES, 0, 0, tiled=True)
    virial = (jnp.sum(lines, axis=0)[:9] * factor).reshape(3, 3)
    return purified, virial


def solution(mesh):
    in_specs = (P(AXES, None, None, None), P(), P(None, AXES, None, None, None))
    out_specs = (P(AXES, None, None, None), P())
    return jax.shard_map(body, mesh=mesh, in_specs=in_specs, out_specs=out_specs, check_vma=False)
```
